256 devices in a mesh: row: 8 (over z_lo, y), col: 32 (over x, z_hi, core).
Axes of the slice: x: 4, y: 4, z: 8 (z_hi: 4, z_lo: 2; z = z_hi * 2 + z_lo), core: 2. Of those that a mesh axis runs over, the one named last changes fastest.
Arguments:
- codes: int32 [2, 2048, 2048], P(None, 'row', 'col'), may hold values from 0 to 255
- codebooks: bfloat16 [2, 256, 8], replicated, may hold values from -3 to 3
- row_scale: float32 [2048], P('row'), may hold values from 0.5 to 2
- initial: bfloat16 [2048, 16384], P('row', 'col'), may hold values from -6 to 6
- hessian: bfloat16 [16384, 16384], P('row', 'col'), as said below
Outputs:
- hessian_product: float32 [2048, 16384], P('row', 'col')
- scale_grad: float32 [2048], P('row')
- codebook_grad: float32 [2, 256, 8], replicated
The draws below stay inside these ranges and needn't reach their ends.
Inputs may be any that keep to these rules, and one draw needn't show every extreme that they name: hessian is exactly symmetric.
All inputs are finite; a program needn't handle non-finite values.
Results may differ from the reference program's by a relative error of at most 0.0029.
Values may be sent and summed in bfloat16 or wider, within the bound.
No kernel may reach another device: no remote copies, remote signals or barrier semaphores. Data moves between devices by JAX's collectives and lax.ppermute only.
A program may use at most 128 MiB of HBM per device.

```python
import math
import jax
import jax.numpy as jnp
from jax import lax

K = 16384
CB = 256
GS = 8
ROWS = 2048
GROUPS = 2048


def draw_hessian(key, part):
    key = jax.random.fold_in(key, 11)
    key_entries, key_scales = jax.random.split(key)
    spread = 1.1
    logs = jax.random.uniform(key_scales, (K,), jnp.float32, 0.0, spread)
    scales = jnp.exp(logs)
    entries = jax.random.normal(key_entries, (K, K), jnp.float32)
    offdiag = (entries + entries.T) * (0.35 / K ** 0.5)
    diagonal = (lax.broadcasted_iota(jnp.int32, (K, K), 0) == lax.broadcasted_iota(jnp.int32, (K, K), 1)).astype(jnp.float32)
    outer = scales[:, None] * scales[None, :]
    return (outer * (offdiag + diagonal)).astype(jnp.bfloat16)


def place_ends(values, key, low, largest):
    longest = values.shape.index(max(values.shape))
    spots = []
    for shift in (0, 1):
        where = [jax.random.randint(jax.random.fold_in(key, axis), (), 0, length) for axis, length in enumerate(values.shape)]
        where[longest] = (where[longest] + shift) % values.shape[longest]
        spots.append(tuple(where))
    return values.at[spots[0]].set(low).at[spots[1]].set(largest)


def shard_levels(stream_key, shape, cuts, low, largest):
    level = 1.0
    for axis_at, shards_of in cuts:
        draws = jax.random.uniform(jax.random.fold_in(jax.random.fold_in(stream_key, 6), axis_at), (shards_of,), jnp.float32, low / len(cuts), largest / len(cuts))
        level = level * jnp.repeat(jnp.exp(draws), shape[axis_at] // shards_of).reshape((-1,) + (1,) * (len(shape) - 1 - axis_at))
    return level


def gaussian(key, dims, width, bound, shards=(), kind=jnp.bfloat16):
    array = jax.random.normal(key, dims, jnp.float32) * width
    if len(shards) > 0:
        array = shard_levels(key, dims, shards, -0.22, 0.18) * array
    return jnp.clip(array, min=-bound, max=bound).astype(kind)


def setup_inputs(seed: int = 0) -> dict:
    keys = jax.random.split(jax.random.key(seed), 6)
    return {
        "codes": place_ends(jax.random.randint(keys[0], (2, ROWS, GROUPS), 0, CB), jax.random.fold_in(keys[0], 1), 0, CB - 1).astype(jnp.int32),
        "codebooks": gaussian(keys[1], (2, CB, GS), 0.5, 3.0),
        "row_scale": jnp.clip(jnp.exp(math.log(2.0) - 1.3862944 * jax.random.uniform(keys[2], (ROWS,), jnp.float32) ** shard_levels(keys[2], (ROWS,), ((0, 8),), -0.2, 0.2)), 0.5, 2.0),
        "initial": gaussian(keys[3], (ROWS, K), 1.0, 6.0, ((0, 8), (1, 32))),
        "hessian": draw_hessian(jax.random.fold_in(keys[5], 71), 0),
    }


def reference(codes, codebooks, row_scale, initial, hessian):
    books = codebooks.astype(jnp.float32)
    first = jnp.take(books[0], codes[0], axis=0)
    second = jnp.take(books[1], codes[1], axis=0)
    unscaled = (first + second).reshape(ROWS, K)
    decoded = row_scale[:, None] * unscaled
    error = (decoded - initial.astype(jnp.float32)).astype(jnp.bfloat16)
    product = 2.0 * jnp.dot(error, hessian, preferred_element_type=jnp.float32)
    scale_grad = jnp.sum(product * unscaled, axis=1) / K
    weighted = (row_scale[:, None] * product).reshape(ROWS * GROUPS, GS)
    grads = [jax.ops.segment_sum(weighted, codes[m].reshape(-1).astype(jnp.int32), num_segments=CB) for m in range(2)]
    codebook_grad = jnp.stack(grads) * (CB / (ROWS * GROUPS))
    return product, scale_grad, codebook_grad
```

```python
import functools

import jax
import jax.numpy as jnp
import numpy as np
from jax import lax
from jax.experimental import pallas as pl
from jax.experimental.pallas import tpu as pltpu
from jax.sharding import Mesh
from jax.sharding import PartitionSpec as P

AXES = ("z_lo", "y", "x", "z_hi", "core")
SIZES = (2, 4, 4, 4, 2)
ROW = ("z_lo", "y")
COL = ("x", "z_hi", "core")
PLACES = np.arange(256).reshape(SIZES)


def route(target):
    pairs = []
    for place in np.ndindex(*SIZES):
        to = tuple(t % n for t, n in zip(target(*place), SIZES))
        pairs.append((int(PLACES[place]), int(PLACES[to])))
    assert len({d for _, d in pairs}) == PLACES.size
    return pairs


def send(a, target):
    return lax.ppermute(a, AXES, route(target))


def to_plane(z_lo, y, x, z_hi, core):
    return (
        z_lo,
        (x % 2) * 2 + z_hi // 2,
        x + y % 2,
        z_hi if y < 2 else 3 - z_hi,
        core,
    )


def ring_x(a):
    return send(a, lambda zl, y, x, zh, c: (zl, y, x + (1 - 2 * c), zh, c))


def ring_z(a):
    return send(a, lambda zl, y, x, zh, c: (zl, y, x, zh + (1 - 2 * c), c))


def swap_core(a):
    return send(a, lambda zl, y, x, zh, c: (zl, y, x, zh, 1 - c))


def matmul_kernel(slots, *refs):
    blocks, (own, across), out, held, h_own, h_across, sem = (
        refs[:4],
        refs[4:6],
        refs[6],
        refs[7],
        refs[8],
        refs[9],
        refs[10],
    )
    copies = [
        pltpu.make_async_copy(own, h_own, sem.at[0]),
        pltpu.make_async_copy(across, h_across, sem.at[1]),
    ]
    n = 0
    for group in blocks:
        for place in range(group.shape[0]):
            for half in range(2):
                slot = slots[n]
                copies.append(
                    pltpu.make_async_copy(
                        group.at[place, half], held.at[slot], sem.at[2 + n]
                    )
                )
                n += 1
    for copy in copies:
        copy.start()
    for copy in copies:
        copy.wait()
    for row in range(4):
        lhs = [held[part * 4 + row] for part in range(8)]
        for side, h in enumerate((h_own, h_across)):
            total = jnp.zeros((128, 512), jnp.float32)
            for part in range(8):
                total += jnp.dot(
                    lhs[part],
                    h[part // 4, pl.ds((part % 4) * 512, 512), :],
                    preferred_element_type=jnp.float32,
                )
            out[row, :, side * 512 : (side + 1) * 512] = total.astype(out.dtype)


def body(codes, codebooks, row_scale, initial, hessian):
    rows, width = initial.shape
    groups = width // 8
    words = codebooks.shape[1]
    z_lo, y, x, z_hi, core = (lax.axis_index(a) for a in AXES)

    hess_far = send(hessian, lambda zl, y, x, zh, c: (1 - zl, y, x, zh, c))
    hess_own = jnp.stack([hessian, hess_far])
    hess_across = swap_core(hess_own)

    labels = lax.broadcasted_iota(jnp.int32, (1, 1, words), 2)
    picks = [(codes[m][:, :, None] == labels).astype(jnp.bfloat16) for m in range(2)]
    unscaled = jnp.einsum("rgk,kt->rgt", picks[0], codebooks[0], preferred_element_type=jnp.float32)
    unscaled = unscaled + jnp.einsum(
        "rgk,kt->rgt", picks[1], codebooks[1], preferred_element_type=jnp.float32
    )
    unscaled = unscaled.reshape(rows, width)
    error = (row_scale[:, None] * unscaled - initial.astype(jnp.float32)).astype(jnp.bfloat16)

    half = rows // 2
    mine = lax.dynamic_slice_in_dim(error, core * half, half, 0)
    other = lax.dynamic_slice_in_dim(error, (1 - core) * half, half, 0)
    same = send(mine, to_plane)
    cross = send(other, lambda zl, y, x, zh, c: to_plane(zl, y, x, zh, c)[:4] + (1 - c,))
    block = jnp.stack([same, cross])

    z1 = ring_z(block)
    z2 = ring_z(z1)
    z3 = ring_z(z2)
    first = jnp.stack([block, z1])
    second = jnp.stack([z2, z3])
    f1 = ring_x(first)
    f2 = ring_x(f1)
    f3 = ring_x(f2)
    s1 = ring_x(second)
    s2 = ring_x(s1)
    s3 = ring_x(s2)
    gathered = [
        jnp.concatenate([first, f1]),
        jnp.concatenate([f2, f3]),
        jnp.concatenate([second, s1]),
        jnp.concatenate([s2, s3]),
    ]
    step = 1 - 2 * core
    slots = []
    for which in range(2):
        for dx in range(4):
            for dz in (2 * which, 2 * which + 1):
                from_x = (x - step * dx) % 4
                from_z = (z_hi - step * dz) % 4
                d = (from_x - y // 2) % 4
                q = (d // 2) ^ z_lo
                upper = (from_z // 2) ^ (y % 2)
                b = (from_z % 2) ^ upper
                source_y = upper * 2 + d % 2
                for side in range(2):
                    part = q * 4 + b * 2 + (core ^ side)
                    slots.append(part * 4 + source_y)
    slots = jnp.stack(slots).astype(jnp.int32)

    partial = pl.pallas_call(
        matmul_kernel,
        out_shape=jax.ShapeDtypeStruct((4, half, 2 * width), jnp.bfloat16),
        in_specs=[pl.BlockSpec(memory_space=pltpu.SMEM)]
        + [pl.BlockSpec(memory_space=pl.ANY)] * 6,
        out_specs=pl.BlockSpec(memory_space=pltpu.VMEM),
        scratch_shapes=[
            pltpu.VMEM((32, half, width), jnp.bfloat16),
            pltpu.VMEM((2, 2048, 512), jnp.bfloat16),
            pltpu.VMEM((2, 2048, 512), jnp.bfloat16),
            pltpu.SemaphoreType.DMA((34,)),
        ],
        compiler_params=pltpu.CompilerParams(vmem_limit_bytes=40 * 2**20),
        cost_estimate=pl.CostEstimate(
            flops=2 * 512 * 4096 * 1024, bytes_accessed=13 * 2**20, transcendentals=0
        ),
        name="matmul",
    )(slots, *gathered, hess_own, hess_across)

    parts = lax.all_to_all(partial, "y", 0, 0, tiled=True)
    summed = jnp.sum(parts.astype(jnp.float32), axis=0)
    kept, given = summed[:, :width], summed[:, width:]
    got = swap_core(given)
    product = 2.0 * jnp.where(
        core == 0, jnp.concatenate([kept, got]), jnp.concatenate([got, kept])
    )

    local_scale = jnp.sum(product * unscaled, axis=1)
    weighted = (row_scale[:, None] * product).reshape(rows, groups, 8)
    local_books = jnp.stack(
        [
            jnp.einsum(
                "rgk,rgt->kt",
                picks[m].astype(jnp.float32),
                weighted,
                precision=lax.Precision.HIGHEST,
            )
            for m in range(2)
        ]
    )
    total = jnp.concatenate([local_books.reshape(-1, 128), local_scale.reshape(-1, 128)])
    total = total + swap_core(total)
    for axis in (2, 3):

        def shifted(by):
            return lambda *place: place[:axis] + (place[axis] + by,) + place[axis + 1 :]

        total = total + send(total, shifted(1)) + send(total, shifted(2)) + send(total, shifted(3))
    scale_total = total[-(rows // 128) :].reshape(rows)
    books = total[: -(rows // 128)]
    books = books + send(books, lambda zl, y, x, zh, c: (1 - zl, y, x, zh, c))
    books = (
        books
        + send(books, lambda zl, y, x, zh, c: (zl, y + 1, x, zh, c))
        + send(books, lambda zl, y, x, zh, c: (zl, y + 2, x, zh, c))
        + send(books, lambda zl, y, x, zh, c: (zl, y + 3, x, zh, c))
    )
    full_width = width * 32
    all_groups = rows * 8 * (full_width // 8)
    scale_grad = scale_total / full_width
    codebook_grad = books.reshape(local_books.shape) * (words / all_groups)
    return (product, scale_grad, codebook_grad)


def solution(mesh):
    grid = Mesh(mesh.devices.reshape(SIZES), AXES)
    in_specs = (P(None, ROW, COL), P(), P(ROW), P(ROW, COL), P(ROW, COL))
    out_specs = (P(ROW, COL), P(ROW), P())
    return jax.shard_map(body, mesh=grid, in_specs=in_specs, out_specs=out_specs, check_vma=False)
```

```python
import jax
import jax.numpy as jnp
import numpy as np
from jax import lax
from jax.experimental import pallas as pl
from jax.experimental.pallas import tpu as pltpu
from jax.sharding import Mesh
from jax.sharding import PartitionSpec as P

AXES = ("z_lo", "y_hi", "y_lo", "x", "z_hi", "core")
SIZES = (2, 2, 2, 4, 4, 2)
ROW = ("z_lo", "y_hi", "y_lo")
COL = ("x", "z_hi", "core")
PLACES = np.arange(256).reshape(SIZES)


def send(a, target):
    pairs = []
    for place in np.ndindex(*SIZES):
        to = tuple(t % n for t, n in zip(target(*place), SIZES))
        pairs.append((int(PLACES[place]), int(PLACES[to])))
    assert len({d for _, d in pairs}) == PLACES.size
    return lax.ppermute(a, AXES, pairs)


def shift(a, axis, by):
    at = AXES.index(axis)
    return send(a, lambda *p: p[:at] + (p[at] + by,) + p[at + 1 :])


def turn(a, axis, by):
    at = AXES.index(axis)
    return send(a, lambda *p: p[:at] + (p[at] + by * (1 - 2 * p[-1]),) + p[at + 1 :])


def to_plane(z_lo, y_hi, y_lo, x, z_hi, core):
    return (x // 2, x % 2, y_lo, x + 2 * z_lo + y_hi, z_hi, core)


def decode_kernel(codes, books, scale, initial, decoded, error):
    picks = [codes[m].T for m in range(2)]
    rows = initial.shape[0]
    for g in range(picks[0].shape[0]):
        for lane in range(0, rows, 128):
            total = None
            for m in range(2):
                word = jnp.broadcast_to(picks[m][g : g + 1, lane : lane + 128], (8, 128))
                low = word & 127
                found = jnp.where(
                    word < 128,
                    jnp.take_along_axis(books[m, :, :128], low, axis=1, mode="promise_in_bounds"),
                    jnp.take_along_axis(books[m, :, 128:], low, axis=1, mode="promise_in_bounds"),
                )
                total = found if total is None else total + found
            decoded[8 * g : 8 * g + 8, lane : lane + 128] = total
    error[...] = (scale[...] * decoded[...].T - initial[...].astype(jnp.float32)).astype(error.dtype)

def decode(codes, codebooks, row_scale, initial):
    rows, width = initial.shape
    return pl.pallas_call(
        decode_kernel,
        out_shape=(jax.ShapeDtypeStruct((width, rows), jnp.float32), jax.ShapeDtypeStruct((rows, width), jnp.bfloat16)),
        in_specs=[pl.BlockSpec(memory_space=pltpu.VMEM)] * 4,
        out_specs=(pl.BlockSpec(memory_space=pltpu.VMEM),) * 2,
        compiler_params=pltpu.CompilerParams(vmem_limit_bytes=16 * 2**20),
        cost_estimate=pl.CostEstimate(flops=2**21, bytes_accessed=2**20, transcendentals=0),
        name="decode",
    )(codes, jnp.swapaxes(codebooks, 1, 2).astype(jnp.float32), row_scale.reshape(rows, 1), initial)

def finish_kernel(core, codes, scale, decoded, kept, got, product, totals):
    half = kept.shape[0]
    first = core[0] == 0
    product[:half] = 2.0 * jnp.where(first, kept[...], got[...])
    product[half:] = 2.0 * jnp.where(first, got[...], kept[...])
    totals[16:17, :] = jnp.sum(product[...].T * decoded[...], axis=0, keepdims=True)
    picks = [codes[m].T.astype(jnp.bfloat16) for m in range(2)]
    rows = product.shape[0]
    words = lax.broadcasted_iota(jnp.int32, (256, rows), 0).astype(jnp.bfloat16)
    group = lax.rem(lax.broadcasted_iota(jnp.int32, (rows, 256), 1), 128) // 8
    sums = jnp.zeros((512, 256), jnp.float32)
    for block in range(product.shape[1] // 128):
        weighted = scale[...] * product[:, block * 128 : (block + 1) * 128]
        high = weighted.astype(jnp.bfloat16)
        low = (weighted - high.astype(jnp.float32)).astype(jnp.bfloat16)
        both = jnp.concatenate([high, low], axis=1)
        for part in range(0, 16, 4):
            lhs = []
            rhs = []
            for g in range(part, part + 4):
                at = block * 16 + g
                lhs.append(jnp.concatenate(
                    [(words == picks[m][at : at + 1, :]).astype(jnp.bfloat16) for m in range(2)], axis=0))
                rhs.append(jnp.where(group == g, both, jnp.zeros_like(both)))
            sums += jnp.dot(jnp.concatenate(lhs, axis=1), jnp.concatenate(rhs, axis=0), preferred_element_type=jnp.float32)
    sums = (sums[:, :128] + sums[:, 128:]).T
    folded = jnp.sum(sums.reshape(16, 8, 512), axis=0)
    totals[0:8, :] = folded[:, :256]
    totals[8:16, :] = folded[:, 256:]

def finish(core, codes, row_scale, decoded, kept, got):
    half, width = kept.shape
    rows = 2 * half
    return pl.pallas_call(
        finish_kernel,
        out_shape=(jax.ShapeDtypeStruct((rows, width), jnp.float32), jax.ShapeDtypeStruct((17, 256), jnp.float32)),
        in_specs=[pl.BlockSpec(memory_space=pltpu.SMEM)] + [pl.BlockSpec(memory_space=pltpu.VMEM)] * 5,
        out_specs=(pl.BlockSpec(memory_space=pltpu.VMEM),) * 2,
        compiler_params=pltpu.CompilerParams(vmem_limit_bytes=24 * 2**20),
        cost_estimate=pl.CostEstimate(flops=2**32, bytes_accessed=2**21, transcendentals=0),
        name="finish",
    )(core.reshape(1), codes, row_scale.reshape(rows, 1), decoded, kept, got)

def matmul_kernel(slots, *refs):
    blocks, tiles = refs[:-9], refs[-9:-5]
    out, held, h_own, h_across, sem = refs[-5:]
    copies = [
        pltpu.make_async_copy(tiles[0], h_own.at[0:2048], sem.at[0]),
        pltpu.make_async_copy(tiles[1], h_own.at[2048:4096], sem.at[1]),
        pltpu.make_async_copy(tiles[2], h_across.at[0:2048], sem.at[2]),
        pltpu.make_async_copy(tiles[3], h_across.at[2048:4096], sem.at[3]),
    ]
    n = 0
    for group in blocks:
        for place in range(group.shape[0]):
            for side in range(2):
                rows = pl.multiple_of(slots[2 * n] * 128, 128)
                columns = pl.multiple_of(slots[2 * n + 1] * 512, 512)
                copies.append(
                    pltpu.make_async_copy(
                        group.at[place, side],
                        held.at[pl.ds(rows, 128), pl.ds(columns, 512)],
                        sem.at[4 + n],
                    )
                )
                n += 1
    for copy in copies:
        copy.start()
    for copy in copies[:2] + copies[4:]:
        copy.wait()
    for side, h in enumerate((h_own, h_across)):
        if side:
            copies[2].wait()
            copies[3].wait()
        total = jnp.dot(held[...], h[...], preferred_element_type=jnp.float32)
        for s in range(4):
            out[s, :, side * 512 : (side + 1) * 512] = total[s * 128 : (s + 1) * 128].astype(
                out.dtype
            )


def body(codes, codebooks, row_scale, initial, hessian):
    rows, width = initial.shape
    words = codebooks.shape[1]
    half = rows // 2
    z_lo, y_hi, y_lo, x, z_hi, core = (lax.axis_index(a) for a in AXES)

    far = send(hessian, lambda zl, yh, yl, x, zh, c: (zl, yh, 1 - yl, x, zh, c))
    across = shift(hessian, "core", 1)

    decoded, error = decode(codes, codebooks, row_scale, initial)

    mine = lax.dynamic_slice_in_dim(error, core * half, half, 0)
    other = lax.dynamic_slice_in_dim(error, (1 - core) * half, half, 0)
    same = send(mine, to_plane)
    cross = send(other, lambda *p: to_plane(*p)[:-1] + (1 - p[-1],))
    block = jnp.stack([same, cross])

    own = block[None]
    z_back, z_on = turn(block, "z_hi", 1), turn(block, "z_hi", -1)
    own_back, own_on = turn(own, "x", 1), turn(own, "x", -1)
    near, z_back, own_back, own_on = lax.optimization_barrier(
        (jnp.stack([z_back, z_on]), z_back, own_back, own_on)
    )
    z_two, own_two = turn(z_back, "z_hi", 1), turn(own_back, "x", 1)
    near_back, near_on = turn(near, "x", 1), turn(near, "x", -1)
    last, own_two, near_back, near_on, far = lax.optimization_barrier(
        (z_two[None], own_two, near_back, near_on, far)
    )
    last_back, last_on = turn(last, "x", 1), turn(last, "x", -1)
    near_two, last_two = turn(near_back, "x", 1), turn(last_back, "x", 1)
    far_across = shift(far, "core", 1)
    wide = (
        (own, own_back, own_on, own_two),
        (near, near_back, near_on, near_two),
        (last, last_back, last_on, last_two),
    )

    step = 1 - 2 * core
    slots = []
    for dzs in ((0,), (1, 3), (2,)):
        for dx in (0, 1, 3, 2):
            for dz in dzs:
                from_x = (x - step * dx) % 4
                from_z = (z_hi - step * dz) % 4
                s = (from_x - 2 * z_lo - y_hi) % 4
                tile = (from_z // 2) ^ y_lo
                for side in range(2):
                    slots += [s, tile * 4 + (from_z % 2) * 2 + (core ^ side)]
    slots = jnp.stack(slots).astype(jnp.int32)

    blocks = [b for group in wide for b in group]
    partial = pl.pallas_call(
        matmul_kernel,
        out_shape=jax.ShapeDtypeStruct((4, half, 2 * width), jnp.bfloat16),
        in_specs=[pl.BlockSpec(memory_space=pltpu.SMEM)]
        + [pl.BlockSpec(memory_space=pl.ANY)] * (len(blocks) + 4),
        out_specs=pl.BlockSpec(memory_space=pltpu.VMEM),
        scratch_shapes=[
            pltpu.VMEM((4 * half, 8 * width), jnp.bfloat16),
            pltpu.VMEM((8 * width, width), jnp.bfloat16),
            pltpu.VMEM((8 * width, width), jnp.bfloat16),
            pltpu.SemaphoreType.DMA((36,)),
        ],
        compiler_params=pltpu.CompilerParams(vmem_limit_bytes=32 * 2**20),
        cost_estimate=pl.CostEstimate(
            flops=2 * 512 * 4096 * 1024, bytes_accessed=13 * 2**20, transcendentals=0
        ),
        name="matmul",
    )(slots, *blocks, hessian, far, across, far_across)

    parts = lax.all_to_all(partial, ("z_lo", "y_hi"), 0, 0, tiled=True)
    summed = jnp.sum(parts.astype(jnp.float32), axis=0)
    kept, given = summed[:, :width], summed[:, width:]
    got = shift(given, "core", 1)
    product, total = finish(core, codes, row_scale, decoded, kept, got)

    total = total + shift(total, "core", 1)
    for axis in ("x", "z_hi"):
        total = total + shift(total, axis, 1) + shift(total, axis, -1) + shift(total, axis, 2)
    scale_total, books = total[16], total[:16]
    books = books + shift(books, "z_lo", 1)
    books = books + shift(books, "y_lo", 1)
    books = books + shift(books, "y_hi", 1)
    full_width = width * 32
    all_groups = rows * 8 * (full_width // 8)
    scale_grad = scale_total / full_width
    codebook_grad = jnp.swapaxes(books.reshape(2, 8, words), 1, 2) * (words / all_groups)
    return (product, scale_grad, codebook_grad)


def solution(mesh):
    grid = Mesh(mesh.devices.reshape(SIZES), AXES)
    in_specs = (P(None, ROW, COL), P(), P(ROW), P(ROW, COL), P(ROW, COL))
    out_specs = (P(ROW, COL), P(ROW), P())
    return jax.shard_map(body, mesh=grid, in_specs=in_specs, out_specs=out_specs, check_vma=False)
```

```python
import jax
import jax.numpy as jnp
import numpy as np
from jax import lax
from jax.experimental import pallas as pl
from jax.experimental.pallas import tpu as pltpu
from jax.sharding import Mesh
from jax.sharding import PartitionSpec as P

AXES = ("z_lo", "y_hi", "y_lo", "x", "z_hi", "core")
SIZES = (2, 2, 2, 4, 4, 2)
ROW = ("z_lo", "y_hi", "y_lo")
COL = ("x", "z_hi", "core")
PLACES = np.arange(256).reshape(SIZES)


def send(a, target):
    pairs = []
    for place in np.ndindex(*SIZES):
        to = tuple(t % n for t, n in zip(target(*place), SIZES))
        pairs.append((int(PLACES[place]), int(PLACES[to])))
    assert len({d for _, d in pairs}) == PLACES.size
    return lax.ppermute(a, AXES, pairs)


def shift(a, axis, by):
    at = AXES.index(axis)
    return send(a, lambda *p: p[:at] + (p[at] + by,) + p[at + 1 :])


def turn(a, axis, by):
    at = AXES.index(axis)
    return send(a, lambda *p: p[:at] + (p[at] + by * (1 - 2 * p[-1]),) + p[at + 1 :])


def to_plane(z_lo, y_hi, y_lo, x, z_hi, core):
    return (x // 2, x % 2, y_lo, x + 2 * z_lo + y_hi, z_hi, core)


def decode_kernel(codes_in, books_in, scale, initial_in, decoded, error, codes, books, initial, sem):
    copies = [
        pltpu.make_async_copy(a, b, sem.at[i])
        for i, (a, b) in enumerate(
            ((codes_in, codes), (books_in, books), (initial_in, initial))
        )
    ]
    for copy in copies:
        copy.start()
    copies[0].wait()
    picks = [codes[m] for m in range(2)]
    copies[1].wait()
    tables = [books[m].astype(jnp.float32) for m in range(2)]
    rows = initial.shape[0]
    for g in range(picks[0].shape[0]):
        for lane in range(0, rows, 128):
            total = None
            for m in range(2):
                word = jnp.broadcast_to(picks[m][g : g + 1, lane : lane + 128], (8, 128))
                low = word & 127
                found = [
                    jnp.take_along_axis(
                        tables[m][:, at : at + 128], low, axis=1, mode="promise_in_bounds"
                    )
                    for at in (0, 128)
                ]
                found = jnp.where(word < 128, *found)
                total = found if total is None else total + found
            decoded[8 * g : 8 * g + 8, lane : lane + 128] = total
    copies[2].wait()
    error[...] = ((scale[...] * decoded[...]).T - initial[...].astype(jnp.float32)).astype(
        error.dtype
    )


def decode(codes, codebooks, row_scale, initial):
    rows, width = initial.shape
    return pl.pallas_call(
        decode_kernel,
        out_shape=(
            jax.ShapeDtypeStruct((width, rows), jnp.float32),
            jax.ShapeDtypeStruct((rows, width), jnp.bfloat16),
        ),
        in_specs=[
            pl.BlockSpec(memory_space=pl.ANY),
            pl.BlockSpec(memory_space=pl.ANY),
            pl.BlockSpec(memory_space=pltpu.VMEM),
            pl.BlockSpec(memory_space=pl.ANY),
        ],
        out_specs=(pl.BlockSpec(memory_space=pltpu.VMEM),) * 2,
        scratch_shapes=[
            pltpu.VMEM(codes.shape, codes.dtype),
            pltpu.VMEM(codebooks.shape, codebooks.dtype),
            pltpu.VMEM(initial.shape, initial.dtype),
            pltpu.SemaphoreType.DMA((3,)),
        ],
        compiler_params=pltpu.CompilerParams(vmem_limit_bytes=60 * 2**20),
        cost_estimate=pl.CostEstimate(flops=2**21, bytes_accessed=2**20, transcendentals=0),
        name="decode",
    )(codes, codebooks, row_scale.reshape(1, rows), initial)


def finish_kernel(core, codes, scale, decoded, kept, got, product, totals):
    half = kept.shape[0]
    first = core[0] == 0
    product[:half] = 2.0 * jnp.where(first, kept[...], got[...])
    product[half:] = 2.0 * jnp.where(first, got[...], kept[...])
    totals[16:17, :] = jnp.sum(product[...].T * decoded[...], axis=0, keepdims=True)
    picks = [codes[m].astype(jnp.bfloat16) for m in range(2)]
    rows = product.shape[0]
    words = lax.broadcasted_iota(jnp.int32, (256, rows), 0).astype(jnp.bfloat16)
    group = lax.rem(lax.broadcasted_iota(jnp.int32, (rows, 256), 1), 128) // 8
    sums = jnp.zeros((512, 256), jnp.float32)
    scales = jnp.broadcast_to(scale[...], (128, rows)).T
    for block in range(product.shape[1] // 128):
        weighted = scales * product[:, block * 128 : (block + 1) * 128]
        high = weighted.astype(jnp.bfloat16)
        low = (weighted - high.astype(jnp.float32)).astype(jnp.bfloat16)
        both = jnp.concatenate([high, low], axis=1)
        for part in range(0, 16, 4):
            lhs = []
            rhs = []
            for g in range(part, part + 4):
                at = block * 16 + g
                lhs.append(jnp.concatenate(
                    [(words == picks[m][at : at + 1, :]).astype(jnp.bfloat16) for m in range(2)], axis=0))
                rhs.append(jnp.where(group == g, both, jnp.zeros_like(both)))
            sums += jnp.dot(jnp.concatenate(lhs, axis=1), jnp.concatenate(rhs, axis=0), preferred_element_type=jnp.float32)
    sums = (sums[:, :128] + sums[:, 128:]).T
    folded = jnp.sum(sums.reshape(16, 8, 512), axis=0)
    totals[0:8, :] = folded[:, :256]
    totals[8:16, :] = folded[:, 256:]

def finish(core, codes, row_scale, decoded, kept, got):
    half, width = kept.shape
    rows = 2 * half
    return pl.pallas_call(
        finish_kernel,
        out_shape=(jax.ShapeDtypeStruct((rows, width), jnp.float32), jax.ShapeDtypeStruct((17, 256), jnp.float32)),
        in_specs=[pl.BlockSpec(memory_space=pltpu.SMEM)] + [pl.BlockSpec(memory_space=pltpu.VMEM)] * 5,
        out_specs=(pl.BlockSpec(memory_space=pltpu.VMEM),) * 2,
        compiler_params=pltpu.CompilerParams(vmem_limit_bytes=24 * 2**20),
        cost_estimate=pl.CostEstimate(flops=2**32, bytes_accessed=2**21, transcendentals=0),
        name="finish",
    )(core.reshape(1), codes, row_scale.reshape(1, rows), decoded, kept, got)

def matmul_kernel(slots, own, far_a, far_b, across, across_a, across_b, *refs):
    blocks = refs[:-3]
    out, held, sem = refs[-3:]
    copies = []
    for group in blocks:
        for place in range(group.shape[0]):
            for side in range(2):
                n = len(copies)
                rows = pl.multiple_of(slots[2 * n] * 128, 128)
                columns = pl.multiple_of(slots[2 * n + 1] * 512, 512)
                copies.append(
                    pltpu.make_async_copy(
                        group.at[place, side],
                        held.at[pl.ds(rows, 128), pl.ds(columns, 512)],
                        sem.at[n],
                    )
                )
    for copy in copies:
        copy.start()
    for copy in copies:
        copy.wait()
    for side, tiles in enumerate(((own, far_a, far_b), (across, across_a, across_b))):
        total = None
        at = 0
        for tile in tiles:
            depth = tile.shape[0]
            term = jnp.dot(
                held[:, at : at + depth], tile[...], preferred_element_type=jnp.float32
            )
            total = term if total is None else total + term
            at += depth
        for s in range(4):
            out[s, :, side * 512 : (side + 1) * 512] = total[s * 128 : (s + 1) * 128].astype(
                out.dtype
            )


def body(codes, codebooks, row_scale, initial, hessian):
    rows, width = initial.shape
    words = codebooks.shape[1]
    codes, codebooks = jnp.swapaxes(codes, 1, 2), jnp.swapaxes(codebooks, 1, 2)
    half = rows // 2
    z_lo, y_hi, y_lo, x, z_hi, core = (lax.axis_index(a) for a in AXES)

    far_a = shift(hessian[:512], "y_lo", 1)
    across = shift(hessian, "core", 1)

    decoded, error = decode(codes, codebooks, row_scale, initial)

    mine = lax.dynamic_slice_in_dim(error, core * half, half, 0)
    other = lax.dynamic_slice_in_dim(error, (1 - core) * half, half, 0)
    same = send(mine, to_plane)
    cross = send(other, lambda *p: to_plane(*p)[:-1] + (1 - p[-1],))
    block = jnp.stack([same, cross])

    rest, block, far_a = lax.optimization_barrier((hessian[512:], block, far_a))
    far_b = shift(rest, "y_lo", 1)

    own = block[None]
    z_back, z_on = turn(block, "z_hi", 1), turn(block, "z_hi", -1)
    own_back, own_on = turn(own, "x", 1), turn(own, "x", -1)
    near, z_back, own_back, own_on = lax.optimization_barrier(
        (jnp.stack([z_back, z_on]), z_back, own_back, own_on)
    )
    z_two, own_two = turn(z_back, "z_hi", 1), turn(own_back, "x", 1)
    near_back, near_on = turn(near, "x", 1), turn(near, "x", -1)
    last = z_two[None]
    last_back, last_on = turn(last, "x", 1), turn(last, "x", -1)
    near_two, last_two = turn(near_back, "x", 1), turn(last_back, "x", 1)
    far_b, *_ = lax.optimization_barrier((far_b, near_back, near_on, z_two, own_two))
    across_a, across_b = shift(far_a, "core", 1), shift(far_b, "core", 1)
    wide = (
        (own, own_back, own_on, own_two),
        (near, near_back, near_on, near_two),
        (last, last_back, last_on, last_two),
    )

    step = 1 - 2 * core
    slots = []
    for dzs in ((0,), (1, 3), (2,)):
        for dx in (0, 1, 3, 2):
            for dz in dzs:
                from_x = (x - step * dx) % 4
                from_z = (z_hi - step * dz) % 4
                s = (from_x - 2 * z_lo - y_hi) % 4
                tile = (from_z // 2) ^ y_lo
                for side in range(2):
                    slots += [s, tile * 4 + (from_z % 2) * 2 + (core ^ side)]
    slots = jnp.stack(slots).astype(jnp.int32)

    blocks = [b for group in wide for b in group]
    partial = pl.pallas_call(
        matmul_kernel,
        out_shape=jax.ShapeDtypeStruct((4, half, 2 * width), jnp.bfloat16),
        in_specs=[pl.BlockSpec(memory_space=pltpu.SMEM)]
        + [pl.BlockSpec(memory_space=pltpu.VMEM)] * 6
        + [pl.BlockSpec(memory_space=pl.ANY)] * len(blocks),
        out_specs=pl.BlockSpec(memory_space=pltpu.VMEM),
        scratch_shapes=[
            pltpu.VMEM((4 * half, 8 * width), jnp.bfloat16),
            pltpu.SemaphoreType.DMA((32,)),
        ],
        compiler_params=pltpu.CompilerParams(vmem_limit_bytes=32 * 2**20),
        cost_estimate=pl.CostEstimate(
            flops=2 * 512 * 4096 * 1024, bytes_accessed=13 * 2**20, transcendentals=0
        ),
        name="matmul",
    )(slots, hessian, far_a, far_b, across, across_a, across_b, *blocks)

    parts = lax.all_to_all(partial, ("z_lo", "y_hi"), 0, 0, tiled=True)
    summed = jnp.sum(parts.astype(jnp.float32), axis=0)
    kept, given = summed[:, :width], summed[:, width:]
    got = shift(given, "core", 1)
    product, total = finish(core, codes, row_scale, decoded, kept, got)

    total = total + shift(total, "core", 1)
    for axis in ("x", "z_hi"):
        total = total + shift(total, axis, 1) + shift(total, axis, -1) + shift(total, axis, 2)
    scale_total, books = total[16], total[:16]
    books = books + shift(books, "z_lo", 1)
    books = books + shift(books, "y_lo", 1)
    books = books + shift(books, "y_hi", 1)
    full_width = width * 32
    all_groups = rows * 8 * (full_width // 8)
    scale_grad = scale_total / full_width
    codebook_grad = jnp.swapaxes(books.reshape(2, 8, words), 1, 2) * (words / all_groups)
    return (product, scale_grad, codebook_grad)


def solution(mesh):
    grid = Mesh(mesh.devices.reshape(SIZES), AXES)
    in_specs = (P(None, ROW, COL), P(), P(ROW), P(ROW, COL), P(ROW, COL))
    out_specs = (P(ROW, COL), P(ROW), P())
    return jax.shard_map(body, mesh=grid, in_specs=in_specs, out_specs=out_specs, check_vma=False)
```

```python
import jax
import jax.numpy as jnp
import numpy as np
from jax import lax
from jax.experimental import pallas as pl
from jax.experimental.pallas import tpu as pltpu
from jax.sharding import Mesh
from jax.sharding import PartitionSpec as P

AXES = ("z_lo", "y_hi", "y_lo", "x", "z_hi", "core")
SIZES = (2, 2, 2, 4, 4, 2)
ROW = ("z_lo", "y_hi", "y_lo")
COL = ("x", "z_hi", "core")
PLACES = np.arange(256).reshape(SIZES)


def send(a, target):
    pairs = []
    for place in np.ndindex(*SIZES):
        to = tuple(t % n for t, n in zip(target(*place), SIZES))
        pairs.append((int(PLACES[place]), int(PLACES[to])))
    assert len({d for _, d in pairs}) == PLACES.size
    return lax.ppermute(a, AXES, pairs)


def shift(a, axis, by):
    at = AXES.index(axis)
    return send(a, lambda *p: p[:at] + (p[at] + by,) + p[at + 1 :])


def turn(a, axis, by):
    at = AXES.index(axis)
    return send(a, lambda *p: p[:at] + (p[at] + by * (1 - 2 * p[-1]),) + p[at + 1 :])


def to_plane(z_lo, y_hi, y_lo, x, z_hi, core):
    return (x // 2, x % 2, y_lo, x + 2 * z_lo + y_hi, z_hi, core)


def decode_kernel(codes_in, books_in, scale, initial_in, decoded, error, codes, books, initial, sem):
    copies = [
        pltpu.make_async_copy(a, b, sem.at[i])
        for i, (a, b) in enumerate(
            ((codes_in, codes), (books_in, books), (initial_in, initial))
        )
    ]
    for copy in copies:
        copy.start()
    copies[0].wait()
    picks = [codes[m] for m in range(2)]
    copies[1].wait()
    tables = [books[m].astype(jnp.float32) for m in range(2)]
    rows = initial.shape[0]
    for g in range(picks[0].shape[0]):
        for lane in range(0, rows, 128):
            total = None
            for m in range(2):
                word = jnp.broadcast_to(picks[m][g : g + 1, lane : lane + 128], (8, 128))
                low = word & 127
                found = [
                    jnp.take_along_axis(
                        tables[m][:, at : at + 128], low, axis=1, mode="promise_in_bounds"
                    )
                    for at in (0, 128)
                ]
                found = jnp.where(word < 128, *found)
                total = found if total is None else total + found
            decoded[8 * g : 8 * g + 8, lane : lane + 128] = total
    copies[2].wait()
    error[...] = ((scale[...] * decoded[...]).T - initial[...].astype(jnp.float32)).astype(
        error.dtype
    )


def decode(codes, codebooks, row_scale, initial):
    rows, width = initial.shape
    return pl.pallas_call(
        decode_kernel,
        out_shape=(
            jax.ShapeDtypeStruct((width, rows), jnp.float32),
            jax.ShapeDtypeStruct((rows, width), jnp.bfloat16),
        ),
        in_specs=[
            pl.BlockSpec(memory_space=pl.ANY),
            pl.BlockSpec(memory_space=pl.ANY),
            pl.BlockSpec(memory_space=pltpu.VMEM),
            pl.BlockSpec(memory_space=pl.ANY),
        ],
        out_specs=(pl.BlockSpec(memory_space=pltpu.VMEM),) * 2,
        scratch_shapes=[
            pltpu.VMEM(codes.shape, codes.dtype),
            pltpu.VMEM(codebooks.shape, codebooks.dtype),
            pltpu.VMEM(initial.shape, initial.dtype),
            pltpu.SemaphoreType.DMA((3,)),
        ],
        compiler_params=pltpu.CompilerParams(vmem_limit_bytes=60 * 2**20),
        cost_estimate=pl.CostEstimate(flops=2**21, bytes_accessed=2**20, transcendentals=0),
        name="decode",
    )(codes, codebooks, row_scale.reshape(1, rows), initial)


def finish_kernel(core, codes, scale, decoded, kept, got, product, totals):
    half = kept.shape[0]
    first = core[0] == 0
    product[:half] = 2.0 * jnp.where(first, kept[...], got[...])
    product[half:] = 2.0 * jnp.where(first, got[...], kept[...])
    rows, width = product.shape
    turned = product[...].T
    totals[16:17, :] = jnp.sum(turned * decoded[...], axis=0, keepdims=True)
    weighted = (turned * scale[...]).reshape(width // 8, 8, rows)
    high = weighted.astype(jnp.bfloat16).astype(jnp.float32)
    both = jnp.concatenate([high, weighted - high], axis=1).astype(jnp.bfloat16)
    picks = [codes[m].astype(jnp.bfloat16) for m in range(2)]
    words = lax.broadcasted_iota(jnp.int32, (256, rows), 0).astype(jnp.bfloat16)
    one, none = jnp.bfloat16(1), jnp.bfloat16(0)
    sums = jnp.zeros((16, 512), jnp.float32)
    for at in range(0, width // 8, 8):
        chosen = [
            jnp.concatenate(
                [
                    jnp.maximum(one - jnp.abs(words - picks[m][g : g + 1, :]), none)
                    for m in range(2)
                ],
                axis=0,
            )
            for g in range(at, at + 8)
        ]
        sums += lax.dot_general(
            jnp.concatenate([both[g] for g in range(at, at + 8)], axis=1),
            jnp.concatenate(chosen, axis=1),
            (((1,), (1,)), ((), ())),
            preferred_element_type=jnp.float32,
        )
    sums = sums[:8] + sums[8:]
    totals[0:8, :] = sums[:, :256]
    totals[8:16, :] = sums[:, 256:]


def finish(core, codes, row_scale, decoded, kept, got):
    half, width = kept.shape
    rows = 2 * half
    return pl.pallas_call(
        finish_kernel,
        out_shape=(jax.ShapeDtypeStruct((rows, width), jnp.float32), jax.ShapeDtypeStruct((17, 256), jnp.float32)),
        in_specs=[pl.BlockSpec(memory_space=pltpu.SMEM)] + [pl.BlockSpec(memory_space=pltpu.VMEM)] * 5,
        out_specs=(pl.BlockSpec(memory_space=pltpu.VMEM),) * 2,
        compiler_params=pltpu.CompilerParams(vmem_limit_bytes=16 * 2**20),
        cost_estimate=pl.CostEstimate(flops=2**32, bytes_accessed=2**21, transcendentals=0),
        name="finish",
    )(core.reshape(1), codes, row_scale.reshape(1, rows), decoded, kept, got)

def matmul_kernel(slots, own, far, across, far_across, *refs):
    blocks = refs[:-4]
    out, held, hess, sem = refs[-4:]
    depth, width = 512, own.shape[1]

    def fetch(part):
        at = part * depth
        tiles = (own, across) if at < own.shape[0] else (far, far_across)
        copies = [
            pltpu.make_async_copy(
                tile.at[pl.ds(at % own.shape[0], depth)],
                hess.at[pl.ds(at, depth), pl.ds(side * width, width)],
                sem.at[2 * part + side],
            )
            for side, tile in enumerate(tiles)
        ]
        for copy in copies:
            copy.start()
        return copies

    parts = hess.shape[0] // depth
    fetched = [fetch(0)]
    copies = []
    for group in blocks:
        for place in range(group.shape[0]):
            for side in range(2):
                n = len(copies)
                rows = pl.multiple_of(slots[2 * n] * 128, 128)
                columns = pl.multiple_of(slots[2 * n + 1] * 512, 512)
                copies.append(
                    pltpu.make_async_copy(
                        group.at[place, side],
                        held.at[pl.ds(rows, 128), pl.ds(columns, 512)],
                        sem.at[2 * parts + n],
                    )
                )
                copies[-1].start()
    fetched += [fetch(part) for part in range(1, parts)]
    for copy in copies:
        copy.wait()
    total = None
    for part in range(parts):
        for copy in fetched[part]:
            copy.wait()
        at = part * depth
        term = jnp.dot(
            held[:, at : at + depth], hess[at : at + depth], preferred_element_type=jnp.float32
        )
        total = term if total is None else total + term
    for s in range(4):
        out[s] = total[s * 128 : (s + 1) * 128].astype(out.dtype)


def body(codes, codebooks, row_scale, initial, hessian):
    rows, width = initial.shape
    words = codebooks.shape[1]
    codes, codebooks = jnp.swapaxes(codes, 1, 2), jnp.swapaxes(codebooks, 1, 2)
    half = rows // 2
    z_lo, y_hi, y_lo, x, z_hi, core = (lax.axis_index(a) for a in AXES)

    across = shift(hessian, "core", 1)

    decoded, error = decode(codes, codebooks, row_scale, initial)

    mine = lax.dynamic_slice_in_dim(error, core * half, half, 0)
    other = lax.dynamic_slice_in_dim(error, (1 - core) * half, half, 0)
    same = send(mine, to_plane)
    cross = send(other, lambda *p: to_plane(*p)[:-1] + (1 - p[-1],))
    block = jnp.stack([same, cross])

    mine, block, across = lax.optimization_barrier((hessian, block, across))
    far = shift(mine, "y_lo", 1)

    own = block[None]
    z_back, z_on = turn(block, "z_hi", 1), turn(block, "z_hi", -1)
    own_back, own_on = turn(own, "x", 1), turn(own, "x", -1)
    own_two = turn(own_back, "x", 1)
    near, own_on, own_two = lax.optimization_barrier(
        (jnp.stack([z_back, z_on]), own_on, own_two)
    )
    near_back, near_on = turn(near, "x", 1), turn(near, "x", -1)
    last = turn(z_back, "z_hi", 1)[None]
    last_back, last_on = turn(last, "x", 1), turn(last, "x", -1)
    near_back, near_on, last_back, last_on = lax.optimization_barrier(
        (near_back, near_on, last_back, last_on)
    )
    near_two, last_two = turn(near_back, "x", 1), turn(last_back, "x", 1)
    far, near_two, last_two = lax.optimization_barrier((far, near_two, last_two))
    far_across = shift(far, "core", 1)
    wide = (
        (own, own_back, own_on, own_two),
        (near, near_back, near_on, near_two),
        (last, last_back, last_on, last_two),
    )

    step = 1 - 2 * core
    slots = []
    for dzs in ((0,), (1, 3), (2,)):
        for dx in (0, 1, 3, 2):
            for dz in dzs:
                from_x = (x - step * dx) % 4
                from_z = (z_hi - step * dz) % 4
                s = (from_x - 2 * z_lo - y_hi) % 4
                tile = (from_z // 2) ^ y_lo
                for side in range(2):
                    slots += [s, tile * 4 + (from_z % 2) * 2 + (core ^ side)]
    slots = jnp.stack(slots).astype(jnp.int32)

    blocks = [b for group in wide for b in group]
    partial = pl.pallas_call(
        matmul_kernel,
        out_shape=jax.ShapeDtypeStruct((4, half, 2 * width), jnp.bfloat16),
        in_specs=[pl.BlockSpec(memory_space=pltpu.SMEM)]
        + [pl.BlockSpec(memory_space=pl.ANY)] * (4 + len(blocks)),
        out_specs=pl.BlockSpec(memory_space=pltpu.VMEM),
        scratch_shapes=[
            pltpu.VMEM((4 * half, 8 * width), jnp.bfloat16),
            pltpu.VMEM((8 * width, 2 * width), jnp.bfloat16),
            pltpu.SemaphoreType.DMA((48,)),
        ],
        compiler_params=pltpu.CompilerParams(vmem_limit_bytes=20 * 2**20),
        cost_estimate=pl.CostEstimate(
            flops=2 * 512 * 4096 * 1024, bytes_accessed=13 * 2**20, transcendentals=0
        ),
        name="matmul",
    )(slots, hessian, far, across, far_across, *blocks)

    parts = lax.all_to_all(partial, ("z_lo", "y_hi"), 0, 0, tiled=True)
    summed = jnp.sum(parts.astype(jnp.float32), axis=0)
    kept, given = summed[:, :width], summed[:, width:]
    got = shift(given, "core", 1)
    product, total = finish(core, codes, row_scale, decoded, kept, got)

    total = total + shift(total, "core", 1)
    for axis in ("x", "z_hi"):
        total = total + shift(total, axis, 1) + shift(total, axis, -1) + shift(total, axis, 2)
    scale_total, books = total[16], total[:16]
    copies = jnp.broadcast_to(books, (8, *books.shape))
    books = jnp.sum(lax.all_to_all(copies, ROW, 0, 0, tiled=True), axis=0)
    full_width = width * 32
    all_groups = rows * 8 * (full_width // 8)
    scale_grad = scale_total / full_width
    codebook_grad = jnp.swapaxes(books.reshape(2, 8, words), 1, 2) * (words / all_groups)
    return (product, scale_grad, codebook_grad)


def solution(mesh):
    grid = Mesh(mesh.devices.reshape(SIZES), AXES)
    in_specs = (P(None, ROW, COL), P(), P(ROW), P(ROW, COL), P(ROW, COL))
    out_specs = (P(ROW, COL), P(ROW), P())
    return jax.shard_map(body, mesh=grid, in_specs=in_specs, out_specs=out_specs, check_vma=False)
```

```python
import jax
import jax.numpy as jnp
import numpy as np
from jax import lax
from jax.experimental import pallas as pl
from jax.experimental.pallas import tpu as pltpu
from jax.sharding import Mesh
from jax.sharding import PartitionSpec as P

AXES = ("z_lo", "y_hi", "y_lo", "x", "z_hi", "core")
SIZES = (2, 2, 2, 4, 4, 2)
ROW = ("z_lo", "y_hi", "y_lo")
COL = ("x", "z_hi", "core")
PLACES = np.arange(256).reshape(SIZES)


def send(a, target):
    pairs = []
    for place in np.ndindex(*SIZES):
        to = tuple(t % n for t, n in zip(target(*place), SIZES))
        pairs.append((int(PLACES[place]), int(PLACES[to])))
    assert len({d for _, d in pairs}) == PLACES.size
    return lax.ppermute(a, AXES, pairs)


def shift(a, axis, by):
    at = AXES.index(axis)
    return send(a, lambda *p: p[:at] + (p[at] + by,) + p[at + 1 :])


def turn(a, axis, by):
    at = AXES.index(axis)
    return send(a, lambda *p: p[:at] + (p[at] + by * (1 - 2 * p[-1]),) + p[at + 1 :])


def to_plane(z_lo, y_hi, y_lo, x, z_hi, core):
    return (x // 2, x % 2, y_lo, x + 2 * z_lo + y_hi, z_hi, core)


def decode_kernel(
    codes_in, books_in, scale, initial_in, decoded, mine, other, codes, books, initial, error, sem
):
    copies = [
        pltpu.make_async_copy(a, b, sem.at[i])
        for i, (a, b) in enumerate(
            ((codes_in, codes), (books_in, books), (initial_in, initial))
        )
    ]
    for copy in copies:
        copy.start()
    copies[0].wait()
    picks = [codes[m] for m in range(2)]
    copies[1].wait()
    tables = [books[m].astype(jnp.float32) for m in range(2)]
    rows = initial.shape[0]
    for g in range(picks[0].shape[0]):
        for lane in range(0, rows, 128):
            total = None
            for m in range(2):
                word = jnp.broadcast_to(picks[m][g : g + 1, lane : lane + 128], (8, 128))
                low = word & 127
                found = [
                    jnp.take_along_axis(
                        tables[m][:, at : at + 128], low, axis=1, mode="promise_in_bounds"
                    )
                    for at in (0, 128)
                ]
                found = jnp.where(word < 128, *found)
                total = found if total is None else total + found
            decoded[8 * g : 8 * g + 8, lane : lane + 128] = total
    copies[2].wait()
    error[...] = (scale[...] * decoded[...]).T - initial[...].astype(jnp.float32)
    half = rows // 2
    core = lax.axis_index("core")
    mine[...] = error[pl.ds(pl.multiple_of(core * half, half), half)].astype(mine.dtype)
    other[...] = error[pl.ds(pl.multiple_of((1 - core) * half, half), half)].astype(mine.dtype)


def decode(codes, codebooks, row_scale, initial):
    rows, width = initial.shape
    return pl.pallas_call(
        decode_kernel,
        out_shape=(
            jax.ShapeDtypeStruct((width, rows), jnp.float32),
            jax.ShapeDtypeStruct((rows // 2, width), jnp.bfloat16),
            jax.ShapeDtypeStruct((rows // 2, width), jnp.bfloat16),
        ),
        in_specs=[
            pl.BlockSpec(memory_space=pl.ANY),
            pl.BlockSpec(memory_space=pl.ANY),
            pl.BlockSpec(memory_space=pltpu.VMEM),
            pl.BlockSpec(memory_space=pl.ANY),
        ],
        out_specs=(pl.BlockSpec(memory_space=pltpu.VMEM),) * 3,
        scratch_shapes=[
            pltpu.VMEM(codes.shape, codes.dtype),
            pltpu.VMEM(codebooks.shape, codebooks.dtype),
            pltpu.VMEM(initial.shape, initial.dtype),
            pltpu.VMEM(initial.shape, jnp.float32),
            pltpu.SemaphoreType.DMA((3,)),
        ],
        compiler_params=pltpu.CompilerParams(vmem_limit_bytes=60 * 2**20),
        cost_estimate=pl.CostEstimate(flops=2**21, bytes_accessed=2**20, transcendentals=0),
        name="decode",
    )(codes, codebooks, row_scale.reshape(1, rows), initial)


def finish_kernel(codes, scale, decoded, kept, got, product, totals):
    half = kept.shape[0]
    first = lax.axis_index("core") == 0
    product[:half] = 2.0 * jnp.where(first, kept[...], got[...])
    product[half:] = 2.0 * jnp.where(first, got[...], kept[...])
    rows, width = product.shape
    turned = product[...].T
    totals[16:17, :] = jnp.sum(turned * decoded[...], axis=0, keepdims=True)
    weighted = (turned * scale[...]).reshape(width // 8, 8, rows)
    high = weighted.astype(jnp.bfloat16).astype(jnp.float32)
    both = jnp.concatenate([high, weighted - high], axis=1).astype(jnp.bfloat16)
    picks = [codes[m].astype(jnp.bfloat16) for m in range(2)]
    words = lax.broadcasted_iota(jnp.int32, (256, rows), 0).astype(jnp.bfloat16)
    one, none = jnp.bfloat16(1), jnp.bfloat16(0)
    sums = jnp.zeros((16, 512), jnp.float32)
    for at in range(0, width // 8, 8):
        chosen = [
            jnp.concatenate(
                [
                    jnp.maximum(one - jnp.abs(words - picks[m][g : g + 1, :]), none)
                    for m in range(2)
                ],
                axis=0,
            )
            for g in range(at, at + 8)
        ]
        sums += lax.dot_general(
            jnp.concatenate([both[g] for g in range(at, at + 8)], axis=1),
            jnp.concatenate(chosen, axis=1),
            (((1,), (1,)), ((), ())),
            preferred_element_type=jnp.float32,
        )
    sums = sums[:8] + sums[8:]
    totals[0:8, :] = sums[:, :256]
    totals[8:16, :] = sums[:, 256:]


def finish(codes, row_scale, decoded, kept, got):
    half, width = kept.shape
    rows = 2 * half
    return pl.pallas_call(
        finish_kernel,
        out_shape=(jax.ShapeDtypeStruct((rows, width), jnp.float32), jax.ShapeDtypeStruct((17, 256), jnp.float32)),
        in_specs=[pl.BlockSpec(memory_space=pltpu.VMEM)] * 5,
        out_specs=(pl.BlockSpec(memory_space=pltpu.VMEM),) * 2,
        compiler_params=pltpu.CompilerParams(vmem_limit_bytes=16 * 2**20),
        cost_estimate=pl.CostEstimate(flops=2**32, bytes_accessed=2**21, transcendentals=0),
        name="finish",
    )(codes, row_scale.reshape(1, rows), decoded, kept, got)

def matmul_kernel(own, far, across, far_across, *refs):
    blocks = refs[:-4]
    out, held, hess, sem = refs[-4:]
    depth, width = 512, own.shape[1]

    def fetch(part):
        at = part * depth
        tiles = (own, across) if at < own.shape[0] else (far, far_across)
        copies = [
            pltpu.make_async_copy(
                tile.at[pl.ds(at % own.shape[0], depth)],
                hess.at[pl.ds(at, depth), pl.ds(side * width, width)],
                sem.at[2 * part + side],
            )
            for side, tile in enumerate(tiles)
        ]
        for copy in copies:
            copy.start()
        return copies

    parts = hess.shape[0] // depth
    fetched = [fetch(0)]
    z_lo, y_hi, y_lo, x, z_hi, core = (lax.axis_index(a) for a in AXES)
    step = 1 - 2 * core
    copies = []
    for at, (dx, dzs) in enumerate((dx, dzs) for dzs in ((0,), (1, 3), (2,)) for dx in (0, 1, 3, 2)):
        for place, dz in enumerate(dzs):
            from_x = (x + 8 - step * dx) % 4
            from_z = (z_hi + 8 - step * dz) % 4
            s = (from_x + 8 - 2 * z_lo - y_hi) % 4
            tile = (from_z // 2 + y_lo) % 2
            for side in range(2):
                n = len(copies)
                part = tile * 4 + (from_z % 2) * 2 + (core + side) % 2
                rows = pl.multiple_of(s * 128, 128)
                columns = pl.multiple_of(part * width, width)
                copies.append(
                    pltpu.make_async_copy(
                        blocks[at].at[place, side],
                        held.at[pl.ds(rows, 128), pl.ds(columns, width)],
                        sem.at[2 * parts + n],
                    )
                )
                copies[-1].start()
    fetched += [fetch(part) for part in range(1, parts)]
    for copy in copies:
        copy.wait()
    total = None
    for part in range(parts):
        for copy in fetched[part]:
            copy.wait()
        at = part * depth
        term = jnp.dot(
            held[:, at : at + depth], hess[at : at + depth], preferred_element_type=jnp.float32
        )
        total = term if total is None else total + term
    for s in range(4):
        out[s] = total[s * 128 : (s + 1) * 128].astype(out.dtype)


def body(codes, codebooks, row_scale, initial, hessian):
    rows, width = initial.shape
    words = codebooks.shape[1]
    codes, codebooks = jnp.swapaxes(codes, 1, 2), jnp.swapaxes(codebooks, 1, 2)
    half = rows // 2

    across = shift(hessian, "core", 1)

    decoded, mine, other = decode(codes, codebooks, row_scale, initial)
    same = send(mine, to_plane)
    cross = send(other, lambda *p: to_plane(*p)[:-1] + (1 - p[-1],))
    block = jnp.stack([same, cross])

    tile, block, across = lax.optimization_barrier((hessian, block, across))
    far = shift(tile, "y_lo", 1)

    own = block[None]
    z_back, z_on = turn(block, "z_hi", 1), turn(block, "z_hi", -1)
    own_back, own_on = turn(own, "x", 1), turn(own, "x", -1)
    own_two = turn(own_back, "x", 1)
    near, own_on, own_two = lax.optimization_barrier(
        (jnp.stack([z_back, z_on]), own_on, own_two)
    )
    near_back, near_on = turn(near, "x", 1), turn(near, "x", -1)
    last = turn(z_back, "z_hi", 1)[None]
    last_back, last_on = turn(last, "x", 1), turn(last, "x", -1)
    near_back, near_on, last_back, last_on = lax.optimization_barrier(
        (near_back, near_on, last_back, last_on)
    )
    near_two, last_two = turn(near_back, "x", 1), turn(last_back, "x", 1)
    far, near_two, last_two = lax.optimization_barrier((far, near_two, last_two))
    far_across = shift(far, "core", 1)
    wide = (
        (own, own_back, own_on, own_two),
        (near, near_back, near_on, near_two),
        (last, last_back, last_on, last_two),
    )

    blocks = [b for group in wide for b in group]
    partial = pl.pallas_call(
        matmul_kernel,
        out_shape=jax.ShapeDtypeStruct((4, half, 2 * width), jnp.bfloat16),
        in_specs=[pl.BlockSpec(memory_space=pl.ANY)] * (4 + len(blocks)),
        out_specs=pl.BlockSpec(memory_space=pltpu.VMEM),
        scratch_shapes=[
            pltpu.VMEM((4 * half, 8 * width), jnp.bfloat16),
            pltpu.VMEM((8 * width, 2 * width), jnp.bfloat16),
            pltpu.SemaphoreType.DMA((48,)),
        ],
        compiler_params=pltpu.CompilerParams(vmem_limit_bytes=20 * 2**20),
        cost_estimate=pl.CostEstimate(
            flops=2 * 512 * 4096 * 1024, bytes_accessed=13 * 2**20, transcendentals=0
        ),
        name="matmul",
    )(hessian, far, across, far_across, *blocks)

    parts = lax.all_to_all(partial, ("z_lo", "y_hi"), 0, 0, tiled=True)
    summed = jnp.sum(parts.astype(jnp.float32), axis=0)
    kept, given = summed[:, :width], summed[:, width:]
    got = shift(given, "core", 1)
    product, total = finish(codes, row_scale, decoded, kept, got)

    total = total + shift(total, "core", 1)
    for axis in ("x", "z_hi"):
        total = total + shift(total, axis, 1) + shift(total, axis, -1) + shift(total, axis, 2)
    scale_total, books = total[16], total[:16]
    copies = jnp.broadcast_to(books, (8, *books.shape))
    books = jnp.sum(lax.all_to_all(copies, ROW, 0, 0, tiled=True), axis=0)
    full_width = width * 32
    all_groups = rows * 8 * (full_width // 8)
    scale_grad = scale_total / full_width
    codebook_grad = jnp.swapaxes(books.reshape(2, 8, words), 1, 2) * (words / all_groups)
    return (product, scale_grad, codebook_grad)


def solution(mesh):
    grid = Mesh(mesh.devices.reshape(SIZES), AXES)
    in_specs = (P(None, ROW, COL), P(), P(ROW), P(ROW, COL), P(ROW, COL))
    out_specs = (P(ROW, COL), P(ROW), P())
    return jax.shard_map(body, mesh=grid, in_specs=in_specs, out_specs=out_specs, check_vma=False)
```

```python
import jax
import jax.numpy as jnp
import numpy as np
from jax import lax
from jax.experimental import pallas as pl
from jax.experimental.pallas import tpu as pltpu
from jax.sharding import Mesh
from jax.sharding import PartitionSpec as P

AXES = ("z_lo", "y_hi", "y_lo", "x", "z_hi", "core")
SIZES = (2, 2, 2, 4, 4, 2)
ROW = ("z_lo", "y_hi", "y_lo")
COL = ("x", "z_hi", "core")
PLACES = np.arange(256).reshape(SIZES)


def send(a, target):
    pairs = []
    for place in np.ndindex(*SIZES):
        to = tuple(t % n for t, n in zip(target(*place), SIZES))
        pairs.append((int(PLACES[place]), int(PLACES[to])))
    assert len({d for _, d in pairs}) == PLACES.size
    return lax.ppermute(a, AXES, pairs)


def shift(a, axis, by):
    at = AXES.index(axis)
    return send(a, lambda *p: p[:at] + (p[at] + by,) + p[at + 1 :])


def turn(a, axis, by):
    at = AXES.index(axis)
    return send(a, lambda *p: p[:at] + (p[at] + by * (1 - 2 * p[-1]),) + p[at + 1 :])


def to_plane(z_lo, y_hi, y_lo, x, z_hi, core):
    return (x // 2, x % 2, y_lo, x + 2 * z_lo + y_hi, z_hi, core)


def decode_kernel(
    codes_in, books_in, scale, initial_in, decoded, mine, other, codes, books, initial, error, sem
):
    copies = [
        pltpu.make_async_copy(a, b, sem.at[i])
        for i, (a, b) in enumerate(
            ((codes_in, codes), (books_in, books), (initial_in, initial))
        )
    ]
    for copy in copies:
        copy.start()
    copies[0].wait()
    picks = [codes[m] for m in range(2)]
    copies[1].wait()
    tables = [books[m].astype(jnp.float32) for m in range(2)]
    rows = initial.shape[0]
    for g in range(picks[0].shape[0]):
        for lane in range(0, rows, 128):
            total = None
            for m in range(2):
                word = jnp.broadcast_to(picks[m][g : g + 1, lane : lane + 128], (8, 128))
                low = word & 127
                found = [
                    jnp.take_along_axis(
                        tables[m][:, at : at + 128], low, axis=1, mode="promise_in_bounds"
                    )
                    for at in (0, 128)
                ]
                found = jnp.where(word < 128, *found)
                total = found if total is None else total + found
            decoded[8 * g : 8 * g + 8, lane : lane + 128] = total
    copies[2].wait()
    error[...] = (scale[...] * decoded[...]).T - initial[...].astype(jnp.float32)
    half = rows // 2
    core = lax.axis_index("core")
    mine[...] = error[pl.ds(pl.multiple_of(core * half, half), half)].astype(mine.dtype)
    other[...] = error[pl.ds(pl.multiple_of((1 - core) * half, half), half)].astype(mine.dtype)


def decode(codes, codebooks, row_scale, initial):
    rows, width = initial.shape
    return pl.pallas_call(
        decode_kernel,
        out_shape=(
            jax.ShapeDtypeStruct((width, rows), jnp.float32),
            jax.ShapeDtypeStruct((rows // 2, width), jnp.bfloat16),
            jax.ShapeDtypeStruct((rows // 2, width), jnp.bfloat16),
        ),
        in_specs=[
            pl.BlockSpec(memory_space=pl.ANY),
            pl.BlockSpec(memory_space=pl.ANY),
            pl.BlockSpec(memory_space=pltpu.VMEM),
            pl.BlockSpec(memory_space=pl.ANY),
        ],
        out_specs=(pl.BlockSpec(memory_space=pltpu.VMEM),) * 3,
        scratch_shapes=[
            pltpu.VMEM(codes.shape, codes.dtype),
            pltpu.VMEM(codebooks.shape, codebooks.dtype),
            pltpu.VMEM(initial.shape, initial.dtype),
            pltpu.VMEM(initial.shape, jnp.float32),
            pltpu.SemaphoreType.DMA((3,)),
        ],
        compiler_params=pltpu.CompilerParams(vmem_limit_bytes=60 * 2**20),
        cost_estimate=pl.CostEstimate(flops=2**21, bytes_accessed=2**20, transcendentals=0),
        name="decode",
    )(codes, codebooks, row_scale.reshape(1, rows), initial)


def finish_kernel(codes, scale, decoded, kept, got, product, totals):
    half = kept.shape[0]
    first = lax.axis_index("core") == 0
    product[:half] = 2.0 * jnp.where(first, kept[...], got[...])
    product[half:] = 2.0 * jnp.where(first, got[...], kept[...])
    rows, width = product.shape
    turned = product[...].T
    totals[16:17, :] = jnp.sum(turned * decoded[...], axis=0, keepdims=True)
    weighted = (turned * scale[...]).reshape(width // 8, 8, rows)
    high = weighted.astype(jnp.bfloat16).astype(jnp.float32)
    both = jnp.concatenate([high, weighted - high], axis=1).astype(jnp.bfloat16)
    picks = [codes[m].astype(jnp.bfloat16) for m in range(2)]
    words = lax.broadcasted_iota(jnp.int32, (256, rows), 0).astype(jnp.bfloat16)
    one, none = jnp.bfloat16(1), jnp.bfloat16(0)
    sums = jnp.zeros((16, 512), jnp.float32)
    for at in range(0, width // 8, 8):
        chosen = [
            jnp.concatenate(
                [
                    jnp.maximum(one - jnp.abs(words - picks[m][g : g + 1, :]), none)
                    for m in range(2)
                ],
                axis=0,
            )
            for g in range(at, at + 8)
        ]
        sums += lax.dot_general(
            jnp.concatenate([both[g] for g in range(at, at + 8)], axis=1),
            jnp.concatenate(chosen, axis=1),
            (((1,), (1,)), ((), ())),
            preferred_element_type=jnp.float32,
        )
    sums = sums[:8] + sums[8:]
    totals[0:8, :] = sums[:, :256]
    totals[8:16, :] = sums[:, 256:]


def finish(codes, row_scale, decoded, kept, got):
    half, width = kept.shape
    rows = 2 * half
    return pl.pallas_call(
        finish_kernel,
        out_shape=(jax.ShapeDtypeStruct((rows, width), jnp.float32), jax.ShapeDtypeStruct((17, 256), jnp.float32)),
        in_specs=[pl.BlockSpec(memory_space=pltpu.VMEM)] * 5,
        out_specs=(pl.BlockSpec(memory_space=pltpu.VMEM),) * 2,
        compiler_params=pltpu.CompilerParams(vmem_limit_bytes=16 * 2**20),
        cost_estimate=pl.CostEstimate(flops=2**32, bytes_accessed=2**21, transcendentals=0),
        name="finish",
    )(codes, row_scale.reshape(1, rows), decoded, kept, got)

def matmul_kernel(own, far, across, far_across, *refs):
    blocks = refs[:-4]
    out, held, hess, sem = refs[-4:]
    depth, width = 512, own.shape[1]

    def fetch(part):
        at = part * depth
        tiles = (own, across) if at < own.shape[0] else (far, far_across)
        copies = [
            pltpu.make_async_copy(
                tile.at[pl.ds(at % own.shape[0], depth)],
                hess.at[pl.ds(at, depth), pl.ds(side * width, width)],
                sem.at[2 * part + side],
            )
            for side, tile in enumerate(tiles)
        ]
        for copy in copies:
            copy.start()
        return copies

    parts = hess.shape[0] // depth
    fetched = [fetch(0)]
    z_lo, y_hi, y_lo, x, z_hi, core = (lax.axis_index(a) for a in AXES)
    step = 1 - 2 * core
    copies = []
    for at, (dx, dzs) in enumerate((dx, dzs) for dzs in ((0,), (1, 3), (2,)) for dx in (0, 1, 3, 2)):
        for place, dz in enumerate(dzs):
            from_x = (x + 8 - step * dx) % 4
            from_z = (z_hi + 8 - step * dz) % 4
            s = (from_x + 8 - 2 * z_lo - y_hi) % 4
            tile = (from_z // 2 + y_lo) % 2
            for side in range(2):
                n = len(copies)
                part = tile * 4 + (from_z % 2) * 2 + (core + side) % 2
                rows = pl.multiple_of(s * 128, 128)
                columns = pl.multiple_of(part * width, width)
                copies.append(
                    pltpu.make_async_copy(
                        blocks[at].at[place, side],
                        held.at[pl.ds(rows, 128), pl.ds(columns, width)],
                        sem.at[2 * parts + n],
                    )
                )
                copies[-1].start()
    fetched += [fetch(part) for part in range(1, parts)]
    for copy in copies:
        copy.wait()
    total = None
    for part in range(parts):
        for copy in fetched[part]:
            copy.wait()
        at = part * depth
        term = jnp.dot(
            held[:, at : at + depth], hess[at : at + depth], preferred_element_type=jnp.float32
        )
        total = term if total is None else total + term
    for s in range(4):
        out[s] = total[s * 128 : (s + 1) * 128].astype(out.dtype)


def body(codes, codebooks, row_scale, initial, hessian):
    rows, width = initial.shape
    words = codebooks.shape[1]
    codes, codebooks = jnp.swapaxes(codes, 1, 2), jnp.swapaxes(codebooks, 1, 2)
    half = rows // 2

    across = shift(hessian, "core", 1)

    decoded, mine, other = decode(codes, codebooks, row_scale, initial)
    same = send(mine, to_plane)
    cross = send(other, lambda *p: to_plane(*p)[:-1] + (1 - p[-1],))
    block = jnp.stack([same, cross])

    tile, block, across = lax.optimization_barrier((hessian, block, across))
    far = shift(tile, "y_lo", 1)

    own = block[None]
    z_back, z_on = turn(block, "z_hi", 1), turn(block, "z_hi", -1)
    own_back, own_on = turn(own, "x", 1), turn(own, "x", -1)
    near, own_back, own_on = lax.optimization_barrier(
        (jnp.stack([z_back, z_on]), own_back, own_on)
    )
    own_two = turn(own_back, "x", 1)
    near_back, near_on = turn(near, "x", 1), turn(near, "x", -1)
    last = turn(z_back, "z_hi", 1)[None]
    last_back, last_on = turn(last, "x", 1), turn(last, "x", -1)
    near_back, near_on, last_back, last_on, own_two, far = lax.optimization_barrier(
        (near_back, near_on, last_back, last_on, own_two, far)
    )
    near_two, last_two = turn(near_back, "x", 1), turn(last_back, "x", 1)
    far_across = shift(far, "core", 1)
    wide = (
        (own, own_back, own_on, own_two),
        (near, near_back, near_on, near_two),
        (last, last_back, last_on, last_two),
    )

    blocks = [b for group in wide for b in group]
    partial = pl.pallas_call(
        matmul_kernel,
        out_shape=jax.ShapeDtypeStruct((4, half, 2 * width), jnp.bfloat16),
        in_specs=[pl.BlockSpec(memory_space=pl.ANY)] * 4
        + [pl.BlockSpec(memory_space=pl.ANY)] * len(blocks),
        out_specs=pl.BlockSpec(memory_space=pltpu.VMEM),
        scratch_shapes=[
            pltpu.VMEM((4 * half, 8 * width), jnp.bfloat16),
            pltpu.VMEM((8 * width, 2 * width), jnp.bfloat16),
            pltpu.SemaphoreType.DMA((48,)),
        ],
        compiler_params=pltpu.CompilerParams(vmem_limit_bytes=20 * 2**20),
        cost_estimate=pl.CostEstimate(
            flops=2 * 512 * 4096 * 1024, bytes_accessed=13 * 2**20, transcendentals=0
        ),
        name="matmul",
    )(hessian, far, across, far_across, *blocks)

    parts = lax.all_to_all(partial, ("z_lo", "y_hi"), 0, 0, tiled=True)
    summed = jnp.sum(parts.astype(jnp.float32), axis=0)
    kept, given = summed[:, :width], summed[:, width:]
    got = shift(given, "core", 1)
    product, total = finish(codes, row_scale, decoded, kept, got)

    total = total + shift(total, "core", 1)
    for axis in ("x", "z_hi"):
        total = total + shift(total, axis, 1) + shift(total, axis, -1) + shift(total, axis, 2)
    scale_total, books = total[16], total[:16]
    copies = jnp.broadcast_to(books, (8, *books.shape))
    books = jnp.sum(lax.all_to_all(copies, ROW, 0, 0, tiled=True), axis=0)
    full_width = width * 32
    all_groups = rows * 8 * (full_width // 8)
    scale_grad = scale_total / full_width
    codebook_grad = jnp.swapaxes(books.reshape(2, 8, words), 1, 2) * (words / all_groups)
    return (product, scale_grad, codebook_grad)


def solution(mesh):
    grid = Mesh(mesh.devices.reshape(SIZES), AXES)
    in_specs = (P(None, ROW, COL), P(), P(ROW), P(ROW, COL), P(ROW, COL))
    out_specs = (P(ROW, COL), P(ROW), P())
    return jax.shard_map(body, mesh=grid, in_specs=in_specs, out_specs=out_specs, check_vma=False)
```

```python
import jax
import jax.numpy as jnp
import numpy as np
from jax import lax
from jax.experimental import pallas as pl
from jax.experimental.pallas import tpu as pltpu
from jax.sharding import Mesh
from jax.sharding import PartitionSpec as P

AXES = ("z_lo", "y_hi", "y_lo", "x", "z_hi", "core")
SIZES = (2, 2, 2, 4, 4, 2)
ROW = ("z_lo", "y_hi", "y_lo")
COL = ("x", "z_hi", "core")
PLACES = np.arange(256).reshape(SIZES)


def send(a, target):
    pairs = []
    for place in np.ndindex(*SIZES):
        to = tuple(t % n for t, n in zip(target(*place), SIZES))
        pairs.append((int(PLACES[place]), int(PLACES[to])))
    assert len({d for _, d in pairs}) == PLACES.size
    return lax.ppermute(a, AXES, pairs)


def shift(a, axis, by):
    at = AXES.index(axis)
    return send(a, lambda *p: p[:at] + (p[at] + by,) + p[at + 1 :])


def turn(a, axis, by):
    at = AXES.index(axis)
    return send(a, lambda *p: p[:at] + (p[at] + by * (1 - 2 * p[-1]),) + p[at + 1 :])


def to_plane(z_lo, y_hi, y_lo, x, z_hi, core):
    return (x // 2, x % 2, y_lo, x + 2 * z_lo + y_hi, z_hi, core)


def decode_kernel(
    codes_in, books_in, scale, initial_in, decoded, mine, other, codes, books, initial, error, sem
):
    copies = [
        pltpu.make_async_copy(a, b, sem.at[i])
        for i, (a, b) in enumerate(
            ((codes_in, codes), (books_in, books), (initial_in, initial))
        )
    ]
    for copy in copies:
        copy.start()
    copies[0].wait()
    picks = [codes[m] for m in range(2)]
    copies[1].wait()
    tables = [books[m].astype(jnp.float32) for m in range(2)]
    rows = initial.shape[0]
    for g in range(picks[0].shape[0]):
        for lane in range(0, rows, 128):
            total = None
            for m in range(2):
                word = jnp.broadcast_to(picks[m][g : g + 1, lane : lane + 128], (8, 128))
                low = word & 127
                found = [
                    jnp.take_along_axis(
                        tables[m][:, at : at + 128], low, axis=1, mode="promise_in_bounds"
                    )
                    for at in (0, 128)
                ]
                found = jnp.where(word < 128, *found)
                total = found if total is None else total + found
            decoded[8 * g : 8 * g + 8, lane : lane + 128] = total
    copies[2].wait()
    error[...] = (scale[...] * decoded[...]).T - initial[...].astype(jnp.float32)
    half = rows // 2
    core = lax.axis_index("core")
    mine[...] = error[pl.ds(pl.multiple_of(core * half, half), half)].astype(mine.dtype)
    other[...] = error[pl.ds(pl.multiple_of((1 - core) * half, half), half)].astype(mine.dtype)


def decode(codes, codebooks, row_scale, initial):
    rows, width = initial.shape
    return pl.pallas_call(
        decode_kernel,
        out_shape=(
            jax.ShapeDtypeStruct((width, rows), jnp.float32),
            jax.ShapeDtypeStruct((rows // 2, width), jnp.bfloat16),
            jax.ShapeDtypeStruct((rows // 2, width), jnp.bfloat16),
        ),
        in_specs=[
            pl.BlockSpec(memory_space=pl.ANY),
            pl.BlockSpec(memory_space=pl.ANY),
            pl.BlockSpec(memory_space=pltpu.VMEM),
            pl.BlockSpec(memory_space=pl.ANY),
        ],
        out_specs=(pl.BlockSpec(memory_space=pltpu.VMEM),) * 3,
        scratch_shapes=[
            pltpu.VMEM(codes.shape, codes.dtype),
            pltpu.VMEM(codebooks.shape, codebooks.dtype),
            pltpu.VMEM(initial.shape, initial.dtype),
            pltpu.VMEM(initial.shape, jnp.float32),
            pltpu.SemaphoreType.DMA((3,)),
        ],
        compiler_params=pltpu.CompilerParams(vmem_limit_bytes=60 * 2**20),
        cost_estimate=pl.CostEstimate(flops=2**21, bytes_accessed=2**20, transcendentals=0),
        name="decode",
    )(codes, codebooks, row_scale.reshape(1, rows), initial)


def finish_kernel(codes, scale, decoded, kept, got, product, totals):
    half = kept.shape[0]
    first = lax.axis_index("core") == 0
    product[:half] = 2.0 * jnp.where(first, kept[...], got[...])
    product[half:] = 2.0 * jnp.where(first, got[...], kept[...])
    rows, width = product.shape
    turned = product[...].T
    totals[16:17, :] = jnp.sum(turned * decoded[...], axis=0, keepdims=True)
    weighted = (turned * scale[...]).reshape(width // 8, 8, rows)
    high = weighted.astype(jnp.bfloat16).astype(jnp.float32)
    both = jnp.concatenate([high, weighted - high], axis=1).astype(jnp.bfloat16)
    picks = [codes[m].astype(jnp.bfloat16) for m in range(2)]
    words = lax.broadcasted_iota(jnp.int32, (256, rows), 0).astype(jnp.bfloat16)
    one, none = jnp.bfloat16(1), jnp.bfloat16(0)
    sums = jnp.zeros((16, 512), jnp.float32)
    for at in range(0, width // 8, 8):
        chosen = [
            jnp.concatenate(
                [
                    jnp.maximum(one - jnp.abs(words - picks[m][g : g + 1, :]), none)
                    for m in range(2)
                ],
                axis=0,
            )
            for g in range(at, at + 8)
        ]
        sums += lax.dot_general(
            jnp.concatenate([both[g] for g in range(at, at + 8)], axis=1),
            jnp.concatenate(chosen, axis=1),
            (((1,), (1,)), ((), ())),
            preferred_element_type=jnp.float32,
        )
    sums = sums[:8] + sums[8:]
    totals[0:8, :] = sums[:, :256]
    totals[8:16, :] = sums[:, 256:]


def finish(codes, row_scale, decoded, kept, got):
    half, width = kept.shape
    rows = 2 * half
    return pl.pallas_call(
        finish_kernel,
        out_shape=(jax.ShapeDtypeStruct((rows, width), jnp.float32), jax.ShapeDtypeStruct((17, 256), jnp.float32)),
        in_specs=[pl.BlockSpec(memory_space=pltpu.VMEM)] * 5,
        out_specs=(pl.BlockSpec(memory_space=pltpu.VMEM),) * 2,
        compiler_params=pltpu.CompilerParams(vmem_limit_bytes=16 * 2**20),
        cost_estimate=pl.CostEstimate(flops=2**32, bytes_accessed=2**21, transcendentals=0),
        name="finish",
    )(codes, row_scale.reshape(1, rows), decoded, kept, got)

DEPTH = 512


def tile_copies(tiles, hess, sem):
    copies = []
    for tile in tiles:
        for at in range(0, tile.shape[0], DEPTH):
            n = len(copies)
            copies.append(
                pltpu.make_async_copy(
                    tile.at[pl.ds(at, DEPTH)], hess.at[pl.ds(n * DEPTH, DEPTH)], sem.at[n]
                )
            )
    return copies


def multiply(held, hess, copies, out):
    total = None
    for n, copy in enumerate(copies):
        copy.wait()
        rows = slice(n * DEPTH, (n + 1) * DEPTH)
        term = jnp.dot(held[:, rows], hess[rows], preferred_element_type=jnp.float32)
        total = term if total is None else total + term
    for s in range(4):
        out[s] = total[s * 128 : (s + 1) * 128].astype(out.dtype)


def first_kernel(own, far, *refs):
    blocks = refs[:-4]
    out, held, hess, sem = refs[-4:]
    width = own.shape[1]
    fetched = tile_copies((own, far), hess, sem)
    fetched[0].start()
    z_lo, y_hi, y_lo, x, z_hi, core = (lax.axis_index(a) for a in AXES)
    step = 1 - 2 * core
    copies = []
    for at, (dx, dzs) in enumerate((dx, dzs) for dzs in ((0,), (1, 3), (2,)) for dx in (0, 1, 3, 2)):
        for place, dz in enumerate(dzs):
            from_x = (x + 8 - step * dx) % 4
            from_z = (z_hi + 8 - step * dz) % 4
            s = (from_x + 8 - 2 * z_lo - y_hi) % 4
            tile = (from_z // 2 + y_lo) % 2
            for side in range(2):
                n = len(copies)
                part = tile * 4 + (from_z % 2) * 2 + (core + side) % 2
                rows = pl.multiple_of(s * 128, 128)
                columns = pl.multiple_of(part * width, width)
                copies.append(
                    pltpu.make_async_copy(
                        blocks[at].at[place, side],
                        held.at[pl.ds(rows, 128), pl.ds(columns, width)],
                        sem.at[len(fetched) + n],
                    )
                )
                copies[-1].start()
    for copy in fetched[1:]:
        copy.start()
    for copy in copies:
        copy.wait()
    multiply(held, hess, fetched, out)


def second_kernel(held, across, far_across, out, hess, sem):
    fetched = tile_copies((across, far_across), hess, sem)
    for copy in fetched:
        copy.start()
    multiply(held, hess, fetched, out)


def body(codes, codebooks, row_scale, initial, hessian):
    rows, width = initial.shape
    words = codebooks.shape[1]
    codes, codebooks = jnp.swapaxes(codes, 1, 2), jnp.swapaxes(codebooks, 1, 2)
    half = rows // 2

    across = shift(hessian, "core", 1)

    decoded, mine, other = decode(codes, codebooks, row_scale, initial)
    same = send(mine, to_plane)
    cross = send(other, lambda *p: to_plane(*p)[:-1] + (1 - p[-1],))
    block = jnp.stack([same, cross])

    tile, block, across = lax.optimization_barrier((hessian, block, across))
    far = shift(tile, "y_lo", 1)

    own = block[None]
    z_back, z_on = turn(block, "z_hi", 1), turn(block, "z_hi", -1)
    own_back, own_on = turn(own, "x", 1), turn(own, "x", -1)
    own_two = turn(own_back, "x", 1)
    near, own_on, own_two = lax.optimization_barrier(
        (jnp.stack([z_back, z_on]), own_on, own_two)
    )
    near_back, near_on = turn(near, "x", 1), turn(near, "x", -1)
    last = turn(z_back, "z_hi", 1)[None]
    last_back, last_on = turn(last, "x", 1), turn(last, "x", -1)
    near_back, near_on, last_back, last_on = lax.optimization_barrier(
        (near_back, near_on, last_back, last_on)
    )
    near_two, last_two = turn(near_back, "x", 1), turn(last_back, "x", 1)
    far, near_two, last_two = lax.optimization_barrier((far, near_two, last_two))
    far_across = shift(far, "core", 1)
    wide = (
        (own, own_back, own_on, own_two),
        (near, near_back, near_on, near_two),
        (last, last_back, last_on, last_two),
    )

    blocks = [b for group in wide for b in group]
    hbm, vmem = pl.BlockSpec(memory_space=pl.ANY), pl.BlockSpec(memory_space=pltpu.VMEM)
    settings = dict(
        compiler_params=pltpu.CompilerParams(vmem_limit_bytes=20 * 2**20),
        cost_estimate=pl.CostEstimate(
            flops=2 * 512 * 4096 * 512, bytes_accessed=8 * 2**20, transcendentals=0
        ),
    )
    sums = jax.ShapeDtypeStruct((4, half, width), jnp.bfloat16)
    kept, held = pl.pallas_call(
        first_kernel,
        out_shape=(sums, jax.ShapeDtypeStruct((4 * half, 8 * width), jnp.bfloat16)),
        in_specs=[hbm] * (2 + len(blocks)),
        out_specs=(vmem, vmem),
        scratch_shapes=[
            pltpu.VMEM((8 * width, width), jnp.bfloat16),
            pltpu.SemaphoreType.DMA((40,)),
        ],
        name="first",
        **settings,
    )(hessian, far, *blocks)
    given = pl.pallas_call(
        second_kernel,
        out_shape=sums,
        in_specs=[vmem, hbm, hbm],
        out_specs=vmem,
        scratch_shapes=[
            pltpu.VMEM((8 * width, width), jnp.bfloat16),
            pltpu.SemaphoreType.DMA((8,)),
        ],
        name="second",
        **settings,
    )(held, across, far_across)

    def owned(partial):
        parts = lax.all_to_all(partial, ("z_lo", "y_hi"), 0, 0, tiled=True)
        return jnp.sum(parts.astype(jnp.float32), axis=0)

    kept, given = lax.optimization_barrier((owned(kept), owned(given)))
    got = shift(given, "core", 1)
    product, total = finish(codes, row_scale, decoded, kept, got)

    total = total + shift(total, "core", 1)
    for axis in ("x", "z_hi"):
        total = total + shift(total, axis, 1) + shift(total, axis, -1) + shift(total, axis, 2)
    scale_total, books = total[16], total[:16]
    copies = jnp.broadcast_to(books, (8, *books.shape))
    books = jnp.sum(lax.all_to_all(copies, ROW, 0, 0, tiled=True), axis=0)
    full_width = width * 32
    all_groups = rows * 8 * (full_width // 8)
    scale_grad = scale_total / full_width
    codebook_grad = jnp.swapaxes(books.reshape(2, 8, words), 1, 2) * (words / all_groups)
    return (product, scale_grad, codebook_grad)


def solution(mesh):
    grid = Mesh(mesh.devices.reshape(SIZES), AXES)
    in_specs = (P(None, ROW, COL), P(), P(ROW), P(ROW, COL), P(ROW, COL))
    out_specs = (P(ROW, COL), P(ROW), P())
    return jax.shard_map(body, mesh=grid, in_specs=in_specs, out_specs=out_specs, check_vma=False)
```

```python
import jax
import jax.numpy as jnp
import numpy as np
from jax import lax
from jax.experimental import pallas as pl
from jax.experimental.pallas import tpu as pltpu
from jax.sharding import Mesh
from jax.sharding import PartitionSpec as P

AXES = ("z_lo", "y_hi", "y_lo", "x", "z_hi", "core")
SIZES = (2, 2, 2, 4, 4, 2)
ROW = ("z_lo", "y_hi", "y_lo")
COL = ("x", "z_hi", "core")
PLACES = np.arange(256).reshape(SIZES)


def send(a, target):
    pairs = []
    for place in np.ndindex(*SIZES):
        to = tuple(t % n for t, n in zip(target(*place), SIZES))
        pairs.append((int(PLACES[place]), int(PLACES[to])))
    assert len({d for _, d in pairs}) == PLACES.size
    return lax.ppermute(a, AXES, pairs)


def shift(a, axis, by):
    at = AXES.index(axis)
    return send(a, lambda *p: p[:at] + (p[at] + by,) + p[at + 1 :])


def turn(a, axis, by):
    at = AXES.index(axis)
    return send(a, lambda *p: p[:at] + (p[at] + by * (1 - 2 * p[-1]),) + p[at + 1 :])


def to_plane(z_lo, y_hi, y_lo, x, z_hi, core):
    return (x // 2, x % 2, y_lo, x + 2 * z_lo + y_hi, z_hi, core)


def decode_kernel(
    codes_in, books_in, scale, initial_in, decoded, mine, other, codes, books, initial, error, sem
):
    copies = [
        pltpu.make_async_copy(a, b, sem.at[i])
        for i, (a, b) in enumerate(
            ((codes_in, codes), (books_in, books), (initial_in, initial))
        )
    ]
    for copy in copies:
        copy.start()
    copies[0].wait()
    picks = [codes[m] for m in range(2)]
    copies[1].wait()
    tables = [books[m].astype(jnp.float32) for m in range(2)]
    rows = initial.shape[0]
    for g in range(picks[0].shape[0]):
        for lane in range(0, rows, 128):
            total = None
            for m in range(2):
                word = jnp.broadcast_to(picks[m][g : g + 1, lane : lane + 128], (8, 128))
                low = word & 127
                found = [
                    jnp.take_along_axis(
                        tables[m][:, at : at + 128], low, axis=1, mode="promise_in_bounds"
                    )
                    for at in (0, 128)
                ]
                found = jnp.where(word < 128, *found)
                total = found if total is None else total + found
            decoded[8 * g : 8 * g + 8, lane : lane + 128] = total
    copies[2].wait()
    error[...] = (scale[...] * decoded[...]).T - initial[...].astype(jnp.float32)
    half = rows // 2
    core = lax.axis_index("core")
    mine[...] = error[pl.ds(pl.multiple_of(core * half, half), half)].astype(mine.dtype)
    other[...] = error[pl.ds(pl.multiple_of((1 - core) * half, half), half)].astype(mine.dtype)


def decode(codes, codebooks, row_scale, initial):
    rows, width = initial.shape
    return pl.pallas_call(
        decode_kernel,
        out_shape=(
            jax.ShapeDtypeStruct((width, rows), jnp.float32),
            jax.ShapeDtypeStruct((rows // 2, width), jnp.bfloat16),
            jax.ShapeDtypeStruct((rows // 2, width), jnp.bfloat16),
        ),
        in_specs=[
            pl.BlockSpec(memory_space=pl.ANY),
            pl.BlockSpec(memory_space=pl.ANY),
            pl.BlockSpec(memory_space=pltpu.VMEM),
            pl.BlockSpec(memory_space=pl.ANY),
        ],
        out_specs=(pl.BlockSpec(memory_space=pltpu.VMEM),) * 3,
        scratch_shapes=[
            pltpu.VMEM(codes.shape, codes.dtype),
            pltpu.VMEM(codebooks.shape, codebooks.dtype),
            pltpu.VMEM(initial.shape, initial.dtype),
            pltpu.VMEM(initial.shape, jnp.float32),
            pltpu.SemaphoreType.DMA((3,)),
        ],
        compiler_params=pltpu.CompilerParams(vmem_limit_bytes=60 * 2**20),
        cost_estimate=pl.CostEstimate(flops=2**21, bytes_accessed=2**20, transcendentals=0),
        name="decode",
    )(codes, codebooks, row_scale.reshape(1, rows), initial)


def finish_kernel(codes, scale, decoded, kept, got, product, totals):
    half = kept.shape[0]
    first = lax.axis_index("core") == 0
    product[:half] = 2.0 * jnp.where(first, kept[...], got[...])
    product[half:] = 2.0 * jnp.where(first, got[...], kept[...])
    rows, width = product.shape
    turned = product[...].T
    totals[16:17, :] = jnp.sum(turned * decoded[...], axis=0, keepdims=True)
    weighted = (turned * scale[...]).reshape(width // 8, 8, rows)
    high = weighted.astype(jnp.bfloat16).astype(jnp.float32)
    both = jnp.concatenate([high, weighted - high], axis=1).astype(jnp.bfloat16)
    picks = [codes[m].astype(jnp.bfloat16) for m in range(2)]
    words = lax.broadcasted_iota(jnp.int32, (256, rows), 0).astype(jnp.bfloat16)
    one, none = jnp.bfloat16(1), jnp.bfloat16(0)
    sums = jnp.zeros((16, 512), jnp.float32)
    for at in range(0, width // 8, 8):
        chosen = [
            jnp.concatenate(
                [
                    jnp.maximum(one - jnp.abs(words - picks[m][g : g + 1, :]), none)
                    for m in range(2)
                ],
                axis=0,
            )
            for g in range(at, at + 8)
        ]
        sums += lax.dot_general(
            jnp.concatenate([both[g] for g in range(at, at + 8)], axis=1),
            jnp.concatenate(chosen, axis=1),
            (((1,), (1,)), ((), ())),
            preferred_element_type=jnp.float32,
        )
    sums = sums[:8] + sums[8:]
    totals[0:8, :] = sums[:, :256]
    totals[8:16, :] = sums[:, 256:]


def finish(codes, row_scale, decoded, kept, got):
    half, width = kept.shape
    rows = 2 * half
    return pl.pallas_call(
        finish_kernel,
        out_shape=(jax.ShapeDtypeStruct((rows, width), jnp.float32), jax.ShapeDtypeStruct((17, 256), jnp.float32)),
        in_specs=[pl.BlockSpec(memory_space=pltpu.VMEM)] * 5,
        out_specs=(pl.BlockSpec(memory_space=pltpu.VMEM),) * 2,
        compiler_params=pltpu.CompilerParams(vmem_limit_bytes=16 * 2**20),
        cost_estimate=pl.CostEstimate(flops=2**32, bytes_accessed=2**21, transcendentals=0),
        name="finish",
    )(codes, row_scale.reshape(1, rows), decoded, kept, got)

DEPTH = 512


def tile_copies(tiles, hess, sem):
    copies = []
    for tile in tiles:
        for at in range(0, tile.shape[0], DEPTH):
            n = len(copies)
            copies.append(
                pltpu.make_async_copy(
                    tile.at[pl.ds(at, DEPTH)], hess.at[pl.ds(n * DEPTH, DEPTH)], sem.at[n]
                )
            )
    return copies


def multiply(held, hess, copies, out, at=0):
    total = None
    for n, copy in enumerate(copies):
        copy.wait()
        rows = slice(n * DEPTH, (n + 1) * DEPTH)
        term = jnp.dot(held[:, rows], hess[rows], preferred_element_type=jnp.float32)
        total = term if total is None else total + term
    for s in range(4):
        out[s, :, at : at + hess.shape[1]] = total[s * 128 : (s + 1) * 128].astype(out.dtype)


def first_kernel(own, far, *refs):
    blocks = refs[:-4]
    out, held, hess, sem = refs[-4:]
    width = own.shape[1]
    fetched = tile_copies((own, far), hess, sem)
    fetched[0].start()
    z_lo, y_hi, y_lo, x, z_hi, core = (lax.axis_index(a) for a in AXES)
    step = 1 - 2 * core
    copies = []
    for at, (dx, dzs) in enumerate((dx, dzs) for dzs in ((0,), (1, 3), (2,)) for dx in (0, 1, 3, 2)):
        for place, dz in enumerate(dzs):
            from_x = (x + 8 - step * dx) % 4
            from_z = (z_hi + 8 - step * dz) % 4
            s = (from_x + 8 - 2 * z_lo - y_hi) % 4
            tile = (from_z // 2 + y_lo) % 2
            for side in range(2):
                n = len(copies)
                part = tile * 4 + (from_z % 2) * 2 + (core + side) % 2
                rows = pl.multiple_of(s * 128, 128)
                columns = pl.multiple_of(part * width, width)
                copies.append(
                    pltpu.make_async_copy(
                        blocks[at].at[place, side],
                        held.at[pl.ds(rows, 128), pl.ds(columns, width)],
                        sem.at[len(fetched) + n],
                    )
                )
                copies[-1].start()
    for copy in fetched[1:]:
        copy.start()
    for copy in copies:
        copy.wait()
    multiply(held, hess, fetched, out)


def second_kernel(kept, held, across, far_across, out, hess, sem):
    fetched = tile_copies((across, far_across), hess, sem)
    for copy in fetched:
        copy.start()
    width = hess.shape[1]
    out[:, :, :width] = kept[...]
    multiply(held, hess, fetched, out, width)


def body(codes, codebooks, row_scale, initial, hessian):
    rows, width = initial.shape
    words = codebooks.shape[1]
    codes, codebooks = jnp.swapaxes(codes, 1, 2), jnp.swapaxes(codebooks, 1, 2)
    half = rows // 2

    across = shift(hessian, "core", 1)

    decoded, mine, other = decode(codes, codebooks, row_scale, initial)
    same = send(mine, to_plane)
    cross = send(other, lambda *p: to_plane(*p)[:-1] + (1 - p[-1],))
    block = jnp.stack([same, cross])

    tile, block, across = lax.optimization_barrier((hessian, block, across))
    far = shift(tile, "y_lo", 1)

    own = block[None]
    z_back, z_on = turn(block, "z_hi", 1), turn(block, "z_hi", -1)
    own_back, own_on = turn(own, "x", 1), turn(own, "x", -1)
    own_two = turn(own_back, "x", 1)
    near, own_on, own_two = lax.optimization_barrier(
        (jnp.stack([z_back, z_on]), own_on, own_two)
    )
    near_back, near_on = turn(near, "x", 1), turn(near, "x", -1)
    last = turn(z_back, "z_hi", 1)[None]
    last_back, last_on = turn(last, "x", 1), turn(last, "x", -1)
    near_on, last_back, last_on, own_two = lax.optimization_barrier((near_on, last_back, last_on, own_two))
    near_two, last_two = turn(near_back, "x", 1), turn(last_back, "x", 1)
    far, near_two, last_two = lax.optimization_barrier((far, near_two, last_two))
    far_across = shift(far, "core", 1)
    wide = (
        (own, own_back, own_on, own_two),
        (near, near_back, near_on, near_two),
        (last, last_back, last_on, last_two),
    )

    blocks = [b for group in wide for b in group]
    hbm, vmem = pl.BlockSpec(memory_space=pl.ANY), pl.BlockSpec(memory_space=pltpu.VMEM)
    settings = dict(
        compiler_params=pltpu.CompilerParams(vmem_limit_bytes=20 * 2**20),
        cost_estimate=pl.CostEstimate(
            flops=2 * 512 * 4096 * 512, bytes_accessed=8 * 2**20, transcendentals=0
        ),
    )
    sums = jax.ShapeDtypeStruct((4, half, width), jnp.bfloat16)
    kept, held = pl.pallas_call(
        first_kernel,
        out_shape=(sums, jax.ShapeDtypeStruct((4 * half, 8 * width), jnp.bfloat16)),
        in_specs=[hbm] * (2 + len(blocks)),
        out_specs=(vmem, vmem),
        scratch_shapes=[
            pltpu.VMEM((8 * width, width), jnp.bfloat16),
            pltpu.SemaphoreType.DMA((40,)),
        ],
        name="first",
        **settings,
    )(hessian, far, *blocks)
    partial = pl.pallas_call(
        second_kernel,
        out_shape=jax.ShapeDtypeStruct((4, half, 2 * width), jnp.bfloat16),
        in_specs=[vmem, vmem, hbm, hbm],
        out_specs=vmem,
        scratch_shapes=[
            pltpu.VMEM((8 * width, width), jnp.bfloat16),
            pltpu.SemaphoreType.DMA((8,)),
        ],
        name="second",
        **settings,
    )(kept, held, across, far_across)

    parts = lax.all_to_all(partial, ("z_lo", "y_hi"), 0, 0, tiled=True)
    summed = jnp.sum(parts.astype(jnp.float32), axis=0)
    kept, given = summed[:, :width], summed[:, width:]
    got = shift(given, "core", 1)
    product, total = finish(codes, row_scale, decoded, kept, got)

    total = total + shift(total, "core", 1)
    for axis in ("x", "z_hi"):
        total = total + shift(total, axis, 1) + shift(total, axis, -1) + shift(total, axis, 2)
    scale_total, books = total[16], total[:16]
    copies = jnp.broadcast_to(books, (8, *books.shape))
    books = jnp.sum(lax.all_to_all(copies, ROW, 0, 0, tiled=True), axis=0)
    full_width = width * 32
    all_groups = rows * 8 * (full_width // 8)
    scale_grad = scale_total / full_width
    codebook_grad = jnp.swapaxes(books.reshape(2, 8, words), 1, 2) * (words / all_groups)
    return (product, scale_grad, codebook_grad)


def solution(mesh):
    grid = Mesh(mesh.devices.reshape(SIZES), AXES)
    in_specs = (P(None, ROW, COL), P(), P(ROW), P(ROW, COL), P(ROW, COL))
    out_specs = (P(ROW, COL), P(ROW), P())
    return jax.shard_map(body, mesh=grid, in_specs=in_specs, out_specs=out_specs, check_vma=False)
```

```python
import jax
import jax.numpy as jnp
import numpy as np
from jax import lax
from jax.experimental import pallas as pl
from jax.experimental.pallas import tpu as pltpu
from jax.sharding import Mesh
from jax.sharding import PartitionSpec as P

AXES = ("z_lo", "y_hi", "y_lo", "x", "z_hi", "core")
SIZES = (2, 2, 2, 4, 4, 2)
ROW = ("z_lo", "y_hi", "y_lo")
COL = ("x", "z_hi", "core")
PLACES = np.arange(256).reshape(SIZES)


def send(a, target):
    pairs = []
    for place in np.ndindex(*SIZES):
        to = tuple(t % n for t, n in zip(target(*place), SIZES))
        pairs.append((int(PLACES[place]), int(PLACES[to])))
    assert len({d for _, d in pairs}) == PLACES.size
    return lax.ppermute(a, AXES, pairs)


def shift(a, axis, by):
    at = AXES.index(axis)
    return send(a, lambda *p: p[:at] + (p[at] + by,) + p[at + 1 :])


def turn(a, axis, by):
    at = AXES.index(axis)
    return send(a, lambda *p: p[:at] + (p[at] + by * (1 - 2 * p[-1]),) + p[at + 1 :])


def to_plane(z_lo, y_hi, y_lo, x, z_hi, core):
    move = {(0, 0): 2, (1, 0): 1, (0, 1): -1, (1, 1): 0}[z_lo ^ (x // 2), y_hi ^ (x % 2)]
    return (x // 2, x % 2, y_lo, x + move, z_hi, core)


def decode_kernel(
    codes_in, books_in, scale, initial_in, decoded, mine, other, codes, books, initial, error, sem
):
    copies = [
        pltpu.make_async_copy(a, b, sem.at[i])
        for i, (a, b) in enumerate(
            ((codes_in, codes), (books_in, books), (initial_in, initial))
        )
    ]
    for copy in copies:
        copy.start()
    copies[0].wait()
    picks = [codes[m] for m in range(2)]
    copies[1].wait()
    tables = [books[m].astype(jnp.float32) for m in range(2)]
    rows = initial.shape[0]
    for g in range(picks[0].shape[0]):
        for lane in range(0, rows, 128):
            total = None
            for m in range(2):
                word = jnp.broadcast_to(picks[m][g : g + 1, lane : lane + 128], (8, 128))
                low = word & 127
                found = [
                    jnp.take_along_axis(
                        tables[m][:, at : at + 128], low, axis=1, mode="promise_in_bounds"
                    )
                    for at in (0, 128)
                ]
                found = jnp.where(word < 128, *found)
                total = found if total is None else total + found
            decoded[8 * g : 8 * g + 8, lane : lane + 128] = total
    copies[2].wait()
    error[...] = (scale[...] * decoded[...]).T - initial[...].astype(jnp.float32)
    half = rows // 2
    core = lax.axis_index("core")
    mine[...] = error[pl.ds(pl.multiple_of(core * half, half), half)].astype(mine.dtype)
    other[...] = error[pl.ds(pl.multiple_of((1 - core) * half, half), half)].astype(mine.dtype)


def decode(codes, codebooks, row_scale, initial):
    rows, width = initial.shape
    return pl.pallas_call(
        decode_kernel,
        out_shape=(
            jax.ShapeDtypeStruct((width, rows), jnp.float32),
            jax.ShapeDtypeStruct((rows // 2, width), jnp.bfloat16),
            jax.ShapeDtypeStruct((rows // 2, width), jnp.bfloat16),
        ),
        in_specs=[
            pl.BlockSpec(memory_space=pl.ANY),
            pl.BlockSpec(memory_space=pl.ANY),
            pl.BlockSpec(memory_space=pltpu.VMEM),
            pl.BlockSpec(memory_space=pl.ANY),
        ],
        out_specs=(pl.BlockSpec(memory_space=pltpu.VMEM),) * 3,
        scratch_shapes=[
            pltpu.VMEM(codes.shape, codes.dtype),
            pltpu.VMEM(codebooks.shape, codebooks.dtype),
            pltpu.VMEM(initial.shape, initial.dtype),
            pltpu.VMEM(initial.shape, jnp.float32),
            pltpu.SemaphoreType.DMA((3,)),
        ],
        compiler_params=pltpu.CompilerParams(vmem_limit_bytes=60 * 2**20),
        cost_estimate=pl.CostEstimate(flops=2**21, bytes_accessed=2**20, transcendentals=0),
        name="decode",
    )(codes, codebooks, row_scale.reshape(1, rows), initial)


def finish_kernel(codes, scale, decoded, own, to_both, to_y, to_z, got, product, totals):
    half, width = got.shape
    kept = own[:, :width]
    for part in (to_both, to_y, to_z):
        kept = kept + part[:, :width].astype(jnp.float32)
    first = lax.axis_index("core") == 0
    product[:half] = 2.0 * jnp.where(first, kept, got[...])
    product[half:] = 2.0 * jnp.where(first, got[...], kept)
    rows, width = product.shape
    turned = product[...].T
    totals[16:17, :] = jnp.sum(turned * decoded[...], axis=0, keepdims=True)
    weighted = (turned * scale[...]).reshape(width // 8, 8, rows)
    high = weighted.astype(jnp.bfloat16).astype(jnp.float32)
    both = jnp.concatenate([high, weighted - high], axis=1).astype(jnp.bfloat16)
    picks = [codes[m].astype(jnp.bfloat16) for m in range(2)]
    words = lax.broadcasted_iota(jnp.int32, (256, rows), 0).astype(jnp.bfloat16)
    one, none = jnp.bfloat16(1), jnp.bfloat16(0)
    sums = jnp.zeros((16, 512), jnp.float32)
    for at in range(0, width // 8, 8):
        chosen = [
            jnp.concatenate(
                [
                    jnp.maximum(one - jnp.abs(words - picks[m][g : g + 1, :]), none)
                    for m in range(2)
                ],
                axis=0,
            )
            for g in range(at, at + 8)
        ]
        sums += lax.dot_general(
            jnp.concatenate([both[g] for g in range(at, at + 8)], axis=1),
            jnp.concatenate(chosen, axis=1),
            (((1,), (1,)), ((), ())),
            preferred_element_type=jnp.float32,
        )
    sums = sums[:8] + sums[8:]
    totals[0:8, :] = sums[:, :256]
    totals[8:16, :] = sums[:, 256:]


def finish(codes, row_scale, decoded, parts, got):
    half, width = got.shape
    rows = 2 * half
    return pl.pallas_call(
        finish_kernel,
        out_shape=(jax.ShapeDtypeStruct((rows, width), jnp.float32), jax.ShapeDtypeStruct((17, 256), jnp.float32)),
        in_specs=[pl.BlockSpec(memory_space=pltpu.VMEM)] * (4 + len(parts)),
        out_specs=(pl.BlockSpec(memory_space=pltpu.VMEM),) * 2,
        compiler_params=pltpu.CompilerParams(vmem_limit_bytes=16 * 2**20),
        cost_estimate=pl.CostEstimate(flops=2**32, bytes_accessed=2**21, transcendentals=0),
        name="finish",
    )(codes, row_scale.reshape(1, rows), decoded, *parts, got)

DEPTH = 512


def tile_copies(tiles, hess, sem):
    copies = []
    for tile in tiles:
        for at in range(0, tile.shape[0], DEPTH):
            n = len(copies)
            copies.append(
                pltpu.make_async_copy(
                    tile.at[pl.ds(at, DEPTH)], hess.at[pl.ds(n * DEPTH, DEPTH)], sem.at[n]
                )
            )
    return copies


def multiply(held, hess, copies):
    total = None
    for n, copy in enumerate(copies):
        copy.wait()
        rows = slice(n * DEPTH, (n + 1) * DEPTH)
        term = jnp.dot(held[:, rows], hess[rows], preferred_element_type=jnp.float32)
        total = term if total is None else total + term
    return total.reshape(4, -1, hess.shape[1])


def first_kernel(own, far, *refs):
    blocks = refs[:-4]
    out, held, hess, sem = refs[-4:]
    width = own.shape[1]
    fetched = tile_copies((own, far), hess, sem)
    fetched[0].start()
    z_lo, y_hi, y_lo, x, z_hi, core = (lax.axis_index(a) for a in AXES)
    step = 1 - 2 * core
    copies = []
    for at, (dx, dzs) in enumerate((dx, dzs) for dzs in ((0,), (1, 3), (2,)) for dx in (0, 1, 3, 2)):
        for place, dz in enumerate(dzs):
            from_x = (x + 8 - step * dx) % 4
            from_z = (z_hi + 8 - step * dz) % 4
            move = (from_x + 8 - 2 * z_lo - y_hi) % 4
            cross_z, cross_y = 1 - move // 2, 1 - (move + 1) % 4 // 2
            s = (z_lo + cross_z) % 2 * 2 + (y_hi + cross_y) % 2
            tile = (from_z // 2 + y_lo) % 2
            for side in range(2):
                n = len(copies)
                part = tile * 4 + (from_z % 2) * 2 + (core + side) % 2
                rows = pl.multiple_of(s * 128, 128)
                columns = pl.multiple_of(part * width, width)
                copies.append(
                    pltpu.make_async_copy(
                        blocks[at].at[place, side],
                        held.at[pl.ds(rows, 128), pl.ds(columns, width)],
                        sem.at[len(fetched) + n],
                    )
                )
                copies[-1].start()
    for copy in fetched[1:]:
        copy.start()
    for copy in copies:
        copy.wait()
    out[...] = multiply(held, hess, fetched)


def second_kernel(kept, held, across, far_across, own, to_y, to_z, to_both, given, hess, sem):
    fetched = tile_copies((across, far_across), hess, sem)
    for copy in fetched:
        copy.start()
    given[...] = multiply(held, hess, fetched)
    width = hess.shape[1]
    z_lo, y_hi = lax.axis_index("z_lo"), lax.axis_index("y_hi")
    for out, s in (
        (own, z_lo * 2 + y_hi),
        (to_y, z_lo * 2 + 1 - y_hi),
        (to_z, (1 - z_lo) * 2 + y_hi),
        (to_both, (1 - z_lo) * 2 + 1 - y_hi),
    ):
        out[:, :width] = kept[s].astype(out.dtype)
        out[:, width:] = given[s].astype(out.dtype)


def body(codes, codebooks, row_scale, initial, hessian):
    rows, width = initial.shape
    words = codebooks.shape[1]
    codes, codebooks = jnp.swapaxes(codes, 1, 2), jnp.swapaxes(codebooks, 1, 2)
    half = rows // 2

    across = shift(hessian, "core", 1)

    decoded, mine, other = decode(codes, codebooks, row_scale, initial)
    same = send(mine, to_plane)
    cross = send(other, lambda *p: to_plane(*p)[:-1] + (1 - p[-1],))
    block = jnp.stack([same, cross])

    tile, block, across = lax.optimization_barrier((hessian, block, across))
    far = shift(tile, "y_lo", 1)

    own = block[None]
    z_back, z_on = turn(block, "z_hi", 1), turn(block, "z_hi", -1)
    own_back, own_on = turn(own, "x", 1), turn(own, "x", -1)
    own_two = turn(own_back, "x", 1)
    near, own_on, own_two = lax.optimization_barrier(
        (jnp.stack([z_back, z_on]), own_on, own_two)
    )
    near_back, near_on = turn(near, "x", 1), turn(near, "x", -1)
    last = turn(z_back, "z_hi", 1)[None]
    last_back, last_on = turn(last, "x", 1), turn(last, "x", -1)
    near_on, last_back, last_on, own_two = lax.optimization_barrier((near_on, last_back, last_on, own_two))
    near_two, last_two = turn(near_back, "x", 1), turn(last_back, "x", 1)
    far, near_two, last_two = lax.optimization_barrier((far, near_two, last_two))
    far_across = shift(far, "core", 1)
    wide = (
        (own, own_back, own_on, own_two),
        (near, near_back, near_on, near_two),
        (last, last_back, last_on, last_two),
    )

    blocks = [b for group in wide for b in group]
    hbm, vmem = pl.BlockSpec(memory_space=pl.ANY), pl.BlockSpec(memory_space=pltpu.VMEM)
    settings = dict(
        compiler_params=pltpu.CompilerParams(vmem_limit_bytes=20 * 2**20),
        cost_estimate=pl.CostEstimate(
            flops=2 * 512 * 4096 * 512, bytes_accessed=8 * 2**20, transcendentals=0
        ),
    )
    kept, held = pl.pallas_call(
        first_kernel,
        out_shape=(
            jax.ShapeDtypeStruct((4, half, width), jnp.float32),
            jax.ShapeDtypeStruct((4 * half, 8 * width), jnp.bfloat16),
        ),
        in_specs=[hbm] * (2 + len(blocks)),
        out_specs=(vmem, vmem),
        scratch_shapes=[
            pltpu.VMEM((8 * width, width), jnp.bfloat16),
            pltpu.SemaphoreType.DMA((40,)),
        ],
        name="first",
        **settings,
    )(hessian, far, *blocks)
    sent = jax.ShapeDtypeStruct((half, 2 * width), jnp.bfloat16)
    own, to_y, to_z, to_both = pl.pallas_call(
        second_kernel,
        out_shape=(jax.ShapeDtypeStruct(sent.shape, jnp.float32), sent, sent, sent),
        in_specs=[vmem, vmem, hbm, hbm],
        out_specs=(vmem,) * 4,
        scratch_shapes=[
            pltpu.VMEM((4, half, width), jnp.float32),
            pltpu.VMEM((8 * width, width), jnp.bfloat16),
            pltpu.SemaphoreType.DMA((8,)),
        ],
        name="second",
        **settings,
    )(kept, held, across, far_across)

    parts = [
        own,
        send(to_both, lambda zl, yh, yl, x, zh, c: (1 - zl, 1 - yh, yl, x, zh, c)),
        shift(to_y, "y_hi", 1),
        shift(to_z, "z_lo", 1),
    ]
    given = sum(part[:, width:].astype(jnp.float32) for part in parts)
    got = shift(given, "core", 1)
    product, total = finish(codes, row_scale, decoded, parts, got)

    total = total + shift(total, "core", 1)
    for axis in ("x", "z_hi"):
        total = total + shift(total, axis, 1) + shift(total, axis, -1) + shift(total, axis, 2)
    scale_total, books = total[16], total[:16]
    copies = jnp.broadcast_to(books, (8, *books.shape))
    books = jnp.sum(lax.all_to_all(copies, ROW, 0, 0, tiled=True), axis=0)
    full_width = width * 32
    all_groups = rows * 8 * (full_width // 8)
    scale_grad = scale_total / full_width
    codebook_grad = jnp.swapaxes(books.reshape(2, 8, words), 1, 2) * (words / all_groups)
    return (product, scale_grad, codebook_grad)


def solution(mesh):
    grid = Mesh(mesh.devices.reshape(SIZES), AXES)
    in_specs = (P(None, ROW, COL), P(), P(ROW), P(ROW, COL), P(ROW, COL))
    out_specs = (P(ROW, COL), P(ROW), P())
    return jax.shard_map(body, mesh=grid, in_specs=in_specs, out_specs=out_specs, check_vma=False)
```

```python
import jax
import jax.numpy as jnp
import numpy as np
from jax import lax
from jax.experimental import pallas as pl
from jax.experimental.pallas import tpu as pltpu
from jax.sharding import Mesh
from jax.sharding import PartitionSpec as P

AXES = ("z_lo", "y_hi", "y_lo", "x", "z_hi", "core")
SIZES = (2, 2, 2, 4, 4, 2)
ROW = ("z_lo", "y_hi", "y_lo")
COL = ("x", "z_hi", "core")
PLACES = np.arange(256).reshape(SIZES)


def send(a, target):
    pairs = []
    for place in np.ndindex(*SIZES):
        to = tuple(t % n for t, n in zip(target(*place), SIZES))
        pairs.append((int(PLACES[place]), int(PLACES[to])))
    assert len({d for _, d in pairs}) == PLACES.size
    return lax.ppermute(a, AXES, pairs)


def shift(a, axis, by):
    at = AXES.index(axis)
    return send(a, lambda *p: p[:at] + (p[at] + by,) + p[at + 1 :])


def turn(a, axis, by):
    at = AXES.index(axis)
    return send(a, lambda *p: p[:at] + (p[at] + by * (1 - 2 * p[-1]),) + p[at + 1 :])


def to_plane(z_lo, y_hi, y_lo, x, z_hi, core):
    return (x // 2, x % 2, y_lo, x + 2 * z_lo + y_hi, z_hi, core)


def decode_kernel(
    codes_in, books_in, scale, initial_in, decoded, mine, other, codes, books, initial, error, sem
):
    copies = [
        pltpu.make_async_copy(a, b, sem.at[i])
        for i, (a, b) in enumerate(
            ((codes_in, codes), (books_in, books), (initial_in, initial))
        )
    ]
    for copy in copies:
        copy.start()
    copies[0].wait()
    picks = [codes[m] for m in range(2)]
    copies[1].wait()
    tables = [books[m].astype(jnp.float32) for m in range(2)]
    rows = initial.shape[0]
    for g in range(picks[0].shape[0]):
        for lane in range(0, rows, 128):
            total = None
            for m in range(2):
                word = jnp.broadcast_to(picks[m][g : g + 1, lane : lane + 128], (8, 128))
                low = word & 127
                found = [
                    jnp.take_along_axis(
                        tables[m][:, at : at + 128], low, axis=1, mode="promise_in_bounds"
                    )
                    for at in (0, 128)
                ]
                found = jnp.where(word < 128, *found)
                total = found if total is None else total + found
            decoded[8 * g : 8 * g + 8, lane : lane + 128] = total
    copies[2].wait()
    error[...] = (scale[...] * decoded[...]).T - initial[...].astype(jnp.float32)
    half = rows // 2
    core = lax.axis_index("core")
    mine[...] = error[pl.ds(pl.multiple_of(core * half, half), half)].astype(mine.dtype)
    other[...] = error[pl.ds(pl.multiple_of((1 - core) * half, half), half)].astype(mine.dtype)


def decode(codes, codebooks, row_scale, initial):
    rows, width = initial.shape
    return pl.pallas_call(
        decode_kernel,
        out_shape=(
            jax.ShapeDtypeStruct((width, rows), jnp.float32),
            jax.ShapeDtypeStruct((rows // 2, width), jnp.bfloat16),
            jax.ShapeDtypeStruct((rows // 2, width), jnp.bfloat16),
        ),
        in_specs=[
            pl.BlockSpec(memory_space=pl.ANY),
            pl.BlockSpec(memory_space=pl.ANY),
            pl.BlockSpec(memory_space=pltpu.VMEM),
            pl.BlockSpec(memory_space=pl.ANY),
        ],
        out_specs=(pl.BlockSpec(memory_space=pltpu.VMEM),) * 3,
        scratch_shapes=[
            pltpu.VMEM(codes.shape, codes.dtype),
            pltpu.VMEM(codebooks.shape, codebooks.dtype),
            pltpu.VMEM(initial.shape, initial.dtype),
            pltpu.VMEM(initial.shape, jnp.float32),
            pltpu.SemaphoreType.DMA((3,)),
        ],
        compiler_params=pltpu.CompilerParams(vmem_limit_bytes=60 * 2**20),
        cost_estimate=pl.CostEstimate(flops=2**21, bytes_accessed=2**20, transcendentals=0),
        name="decode",
    )(codes, codebooks, row_scale.reshape(1, rows), initial)


def finish_kernel(codes, scale, decoded, own, to_both, to_y, to_z, got, product, totals):
    half, width = got.shape
    kept = own[:, :width]
    for part in (to_both, to_y, to_z):
        kept = kept + part[:, :width].astype(jnp.float32)
    first = lax.axis_index("core") == 0
    product[:half] = 2.0 * jnp.where(first, kept, got[...])
    product[half:] = 2.0 * jnp.where(first, got[...], kept)
    rows, width = product.shape
    turned = product[...].T
    totals[16:17, :] = jnp.sum(turned * decoded[...], axis=0, keepdims=True)
    weighted = (turned * scale[...]).reshape(width // 8, 8, rows)
    high = weighted.astype(jnp.bfloat16).astype(jnp.float32)
    both = jnp.concatenate([high, weighted - high], axis=1).astype(jnp.bfloat16)
    picks = [codes[m].astype(jnp.bfloat16) for m in range(2)]
    words = lax.broadcasted_iota(jnp.int32, (256, rows), 0).astype(jnp.bfloat16)
    one, none = jnp.bfloat16(1), jnp.bfloat16(0)
    sums = jnp.zeros((16, 512), jnp.float32)
    for at in range(0, width // 8, 8):
        chosen = [
            jnp.concatenate(
                [
                    jnp.maximum(one - jnp.abs(words - picks[m][g : g + 1, :]), none)
                    for m in range(2)
                ],
                axis=0,
            )
            for g in range(at, at + 8)
        ]
        sums += lax.dot_general(
            jnp.concatenate([both[g] for g in range(at, at + 8)], axis=1),
            jnp.concatenate(chosen, axis=1),
            (((1,), (1,)), ((), ())),
            preferred_element_type=jnp.float32,
        )
    sums = sums[:8] + sums[8:]
    totals[0:8, :] = sums[:, :256]
    totals[8:16, :] = sums[:, 256:]


def finish(codes, row_scale, decoded, parts, got):
    half, width = got.shape
    rows = 2 * half
    return pl.pallas_call(
        finish_kernel,
        out_shape=(jax.ShapeDtypeStruct((rows, width), jnp.float32), jax.ShapeDtypeStruct((17, 256), jnp.float32)),
        in_specs=[pl.BlockSpec(memory_space=pltpu.VMEM)] * (4 + len(parts)),
        out_specs=(pl.BlockSpec(memory_space=pltpu.VMEM),) * 2,
        compiler_params=pltpu.CompilerParams(vmem_limit_bytes=16 * 2**20),
        cost_estimate=pl.CostEstimate(flops=2**32, bytes_accessed=2**21, transcendentals=0),
        name="finish",
    )(codes, row_scale.reshape(1, rows), decoded, *parts, got)

DEPTH = 512


def tile_copies(tiles, hess, sem):
    copies = []
    for tile in tiles:
        for at in range(0, tile.shape[0], DEPTH):
            n = len(copies)
            copies.append(
                pltpu.make_async_copy(
                    tile.at[pl.ds(at, DEPTH)], hess.at[pl.ds(n * DEPTH, DEPTH)], sem.at[n]
                )
            )
    return copies


def multiply(held, hess, copies):
    total = None
    for n, copy in enumerate(copies):
        copy.wait()
        rows = slice(n * DEPTH, (n + 1) * DEPTH)
        term = jnp.dot(held[:, rows], hess[rows], preferred_element_type=jnp.float32)
        total = term if total is None else total + term
    return total.reshape(4, -1, hess.shape[1])


def first_kernel(own, far, *refs):
    blocks = refs[:-4]
    out, held, hess, sem = refs[-4:]
    width = own.shape[1]
    fetched = tile_copies((own, far), hess, sem)
    fetched[0].start()
    z_lo, y_hi, y_lo, x, z_hi, core = (lax.axis_index(a) for a in AXES)
    step = 1 - 2 * core
    copies = []
    for at, (dx, dzs) in enumerate((dx, dzs) for dzs in ((0,), (1, 3), (2,)) for dx in (0, 1, 3, 2)):
        for place, dz in enumerate(dzs):
            from_x = (x + 8 - step * dx) % 4
            from_z = (z_hi + 8 - step * dz) % 4
            s = (from_x + 8 - 2 * z_lo - y_hi) % 4
            tile = (from_z // 2 + y_lo) % 2
            for side in range(2):
                n = len(copies)
                part = tile * 4 + (from_z % 2) * 2 + (core + side) % 2
                rows = pl.multiple_of(s * 128, 128)
                columns = pl.multiple_of(part * width, width)
                copies.append(
                    pltpu.make_async_copy(
                        blocks[at].at[place, side],
                        held.at[pl.ds(rows, 128), pl.ds(columns, width)],
                        sem.at[len(fetched) + n],
                    )
                )
                copies[-1].start()
    for copy in fetched[1:]:
        copy.start()
    for copy in copies:
        copy.wait()
    out[...] = multiply(held, hess, fetched)


def second_kernel(kept, held, across, far_across, own, to_y, to_z, to_both, given, hess, sem):
    fetched = tile_copies((across, far_across), hess, sem)
    for copy in fetched:
        copy.start()
    given[...] = multiply(held, hess, fetched)
    width = hess.shape[1]
    z_lo, y_hi = lax.axis_index("z_lo"), lax.axis_index("y_hi")
    for out, s in (
        (own, z_lo * 2 + y_hi),
        (to_y, z_lo * 2 + 1 - y_hi),
        (to_z, (1 - z_lo) * 2 + y_hi),
        (to_both, (1 - z_lo) * 2 + 1 - y_hi),
    ):
        out[:, :width] = kept[s].astype(out.dtype)
        out[:, width:] = given[s].astype(out.dtype)


def body(codes, codebooks, row_scale, initial, hessian):
    rows, width = initial.shape
    words = codebooks.shape[1]
    codes, codebooks = jnp.swapaxes(codes, 1, 2), jnp.swapaxes(codebooks, 1, 2)
    half = rows // 2

    across = shift(hessian, "core", 1)

    decoded, mine, other = decode(codes, codebooks, row_scale, initial)
    same = send(mine, to_plane)
    cross = send(other, lambda *p: to_plane(*p)[:-1] + (1 - p[-1],))
    block = jnp.stack([same, cross])

    tile, block, across = lax.optimization_barrier((hessian, block, across))
    far = shift(tile, "y_lo", 1)

    own = block[None]
    z_back, z_on = turn(block, "z_hi", 1), turn(block, "z_hi", -1)
    own_back, own_on = turn(own, "x", 1), turn(own, "x", -1)
    own_two = turn(own_back, "x", 1)
    near, own_on, own_two = lax.optimization_barrier(
        (jnp.stack([z_back, z_on]), own_on, own_two)
    )
    near_back, near_on = turn(near, "x", 1), turn(near, "x", -1)
    last = turn(z_back, "z_hi", 1)[None]
    last_back, last_on = turn(last, "x", 1), turn(last, "x", -1)
    near_on, last_back, last_on, own_two = lax.optimization_barrier((near_on, last_back, last_on, own_two))
    near_two, last_two = turn(near_back, "x", 1), turn(last_back, "x", 1)
    far, near_two, last_two = lax.optimization_barrier((far, near_two, last_two))
    far_across = shift(far, "core", 1)
    wide = (
        (own, own_back, own_on, own_two),
        (near, near_back, near_on, near_two),
        (last, last_back, last_on, last_two),
    )

    blocks = [b for group in wide for b in group]
    hbm, vmem = pl.BlockSpec(memory_space=pl.ANY), pl.BlockSpec(memory_space=pltpu.VMEM)
    settings = dict(
        compiler_params=pltpu.CompilerParams(vmem_limit_bytes=20 * 2**20),
        cost_estimate=pl.CostEstimate(
            flops=2 * 512 * 4096 * 512, bytes_accessed=8 * 2**20, transcendentals=0
        ),
    )
    kept, held = pl.pallas_call(
        first_kernel,
        out_shape=(
            jax.ShapeDtypeStruct((4, half, width), jnp.float32),
            jax.ShapeDtypeStruct((4 * half, 8 * width), jnp.bfloat16),
        ),
        in_specs=[hbm] * (2 + len(blocks)),
        out_specs=(vmem, vmem),
        scratch_shapes=[
            pltpu.VMEM((8 * width, width), jnp.bfloat16),
            pltpu.SemaphoreType.DMA((40,)),
        ],
        name="first",
        **settings,
    )(pltpu.with_memory_space_constraint(hessian, pltpu.HBM), far, *blocks)
    sent = jax.ShapeDtypeStruct((half, 2 * width), jnp.bfloat16)
    own, to_y, to_z, to_both = pl.pallas_call(
        second_kernel,
        out_shape=(jax.ShapeDtypeStruct(sent.shape, jnp.float32), sent, sent, sent),
        in_specs=[vmem, vmem, hbm, hbm],
        out_specs=(vmem,) * 4,
        scratch_shapes=[
            pltpu.VMEM((4, half, width), jnp.float32),
            pltpu.VMEM((8 * width, width), jnp.bfloat16),
            pltpu.SemaphoreType.DMA((8,)),
        ],
        name="second",
        **settings,
    )(kept, held, across, far_across)

    parts = [
        own,
        send(to_both, lambda zl, yh, yl, x, zh, c: (1 - zl, 1 - yh, yl, x, zh, c)),
        shift(to_y, "y_hi", 1),
        shift(to_z, "z_lo", 1),
    ]
    given = sum(part[:, width:].astype(jnp.float32) for part in parts)
    got = shift(given, "core", 1)
    product, total = finish(codes, row_scale, decoded, parts, got)

    total = total + shift(total, "core", 1)
    total = total + shift(total, "x", 1) + shift(total, "x", -1) + shift(total, "x", 2)
    copies = jnp.broadcast_to(total, (8, *total.shape))
    copies = lax.all_to_all(copies, ("z_hi", "z_lo"), 0, 0, tiled=True)
    scales = copies[:, 16].reshape(4, 2, rows)
    scale_total = jnp.sum(jnp.where(lax.axis_index("z_lo") == 0, scales[:, 0], scales[:, 1]), axis=0)
    books = jnp.sum(copies[:, :16], axis=0)
    beside, across_y = shift(books, "y_lo", 1), shift(books, "y_hi", 1)
    both = send(books, lambda zl, yh, yl, x, zh, c: (zl, 1 - yh, 1 - yl, x, zh, c))
    books = books + beside + across_y + both
    full_width = width * 32
    all_groups = rows * 8 * (full_width // 8)
    scale_grad = scale_total / full_width
    codebook_grad = jnp.swapaxes(books.reshape(2, 8, words), 1, 2) * (words / all_groups)
    return (product, scale_grad, codebook_grad)


def solution(mesh):
    grid = Mesh(mesh.devices.reshape(SIZES), AXES)
    in_specs = (P(None, ROW, COL), P(), P(ROW), P(ROW, COL), P(ROW, COL))
    out_specs = (P(ROW, COL), P(ROW), P())
    return jax.shard_map(body, mesh=grid, in_specs=in_specs, out_specs=out_specs, check_vma=False)
```

```python
import jax
import jax.numpy as jnp
import numpy as np
from jax import lax
from jax.experimental import pallas as pl
from jax.experimental.pallas import tpu as pltpu
from jax.sharding import Mesh
from jax.sharding import PartitionSpec as P

AXES = ("z_lo", "y_hi", "y_lo", "x", "z_hi", "core")
SIZES = (2, 2, 2, 4, 4, 2)
ROW = ("z_lo", "y_hi", "y_lo")
COL = ("x", "z_hi", "core")
PLACES = np.arange(256).reshape(SIZES)


def send(a, target):
    pairs = []
    for place in np.ndindex(*SIZES):
        to = tuple(t % n for t, n in zip(target(*place), SIZES))
        pairs.append((int(PLACES[place]), int(PLACES[to])))
    assert len({d for _, d in pairs}) == PLACES.size
    return lax.ppermute(a, AXES, pairs)


def shift(a, axis, by):
    at = AXES.index(axis)
    return send(a, lambda *p: p[:at] + (p[at] + by,) + p[at + 1 :])


def turn(a, axis, by):
    at = AXES.index(axis)
    return send(a, lambda *p: p[:at] + (p[at] + by * (1 - 2 * p[-1]),) + p[at + 1 :])


def to_plane(z_lo, y_hi, y_lo, x, z_hi, core):
    return (x // 2, x % 2, y_lo, x + 2 * z_lo + y_hi, z_hi, core)


def decode_kernel(
    codes_in, books_in, scale, initial_in, decoded, mine, other, codes, books, initial, error, sem
):
    copies = [
        pltpu.make_async_copy(a, b, sem.at[i])
        for i, (a, b) in enumerate(
            ((codes_in, codes), (books_in, books), (initial_in, initial))
        )
    ]
    for copy in copies:
        copy.start()
    copies[0].wait()
    picks = [codes[m] for m in range(2)]
    copies[1].wait()
    tables = [books[m].astype(jnp.float32) for m in range(2)]
    rows = initial.shape[0]
    for g in range(picks[0].shape[0]):
        for lane in range(0, rows, 128):
            total = None
            for m in range(2):
                word = jnp.broadcast_to(picks[m][g : g + 1, lane : lane + 128], (8, 128))
                low = word & 127
                found = [
                    jnp.take_along_axis(
                        tables[m][:, at : at + 128], low, axis=1, mode="promise_in_bounds"
                    )
                    for at in (0, 128)
                ]
                found = jnp.where(word < 128, *found)
                total = found if total is None else total + found
            decoded[8 * g : 8 * g + 8, lane : lane + 128] = total
    copies[2].wait()
    error[...] = (scale[...] * decoded[...]).T - initial[...].astype(jnp.float32)
    half = rows // 2
    core = lax.axis_index("core")
    mine[...] = error[pl.ds(pl.multiple_of(core * half, half), half)].astype(mine.dtype)
    other[...] = error[pl.ds(pl.multiple_of((1 - core) * half, half), half)].astype(mine.dtype)


def decode(codes, codebooks, row_scale, initial):
    rows, width = initial.shape
    return pl.pallas_call(
        decode_kernel,
        out_shape=(
            jax.ShapeDtypeStruct((width, rows), jnp.float32),
            jax.ShapeDtypeStruct((rows // 2, width), jnp.bfloat16),
            jax.ShapeDtypeStruct((rows // 2, width), jnp.bfloat16),
        ),
        in_specs=[
            pl.BlockSpec(memory_space=pl.ANY),
            pl.BlockSpec(memory_space=pl.ANY),
            pl.BlockSpec(memory_space=pltpu.VMEM),
            pl.BlockSpec(memory_space=pl.ANY),
        ],
        out_specs=(pl.BlockSpec(memory_space=pltpu.VMEM),) * 3,
        scratch_shapes=[
            pltpu.VMEM(codes.shape, codes.dtype),
            pltpu.VMEM(codebooks.shape, codebooks.dtype),
            pltpu.VMEM(initial.shape, initial.dtype),
            pltpu.VMEM(initial.shape, jnp.float32),
            pltpu.SemaphoreType.DMA((3,)),
        ],
        compiler_params=pltpu.CompilerParams(vmem_limit_bytes=60 * 2**20),
        cost_estimate=pl.CostEstimate(flops=2**21, bytes_accessed=2**20, transcendentals=0),
        name="decode",
    )(codes, codebooks, row_scale.reshape(1, rows), initial)


def finish_kernel(codes, scale, decoded, own, to_both, to_y, to_z, got, product, totals):
    half, width = got.shape
    kept = own[:, :width]
    for part in (to_both, to_y, to_z):
        kept = kept + part[:, :width].astype(jnp.float32)
    first = lax.axis_index("core") == 0
    product[:half] = 2.0 * jnp.where(first, kept, got[...])
    product[half:] = 2.0 * jnp.where(first, got[...], kept)
    rows, width = product.shape
    turned = product[...].T
    totals[16:17, :] = jnp.sum(turned * decoded[...], axis=0, keepdims=True)
    weighted = (turned * scale[...]).reshape(width // 8, 8, rows)
    high = weighted.astype(jnp.bfloat16).astype(jnp.float32)
    both = jnp.concatenate([high, weighted - high], axis=1).astype(jnp.bfloat16)
    picks = [codes[m].astype(jnp.bfloat16) for m in range(2)]
    words = lax.broadcasted_iota(jnp.int32, (256, rows), 0).astype(jnp.bfloat16)
    one, none = jnp.bfloat16(1), jnp.bfloat16(0)
    sums = jnp.zeros((16, 512), jnp.float32)
    for at in range(0, width // 8, 8):
        chosen = [
            jnp.concatenate(
                [
                    jnp.maximum(one - jnp.abs(words - picks[m][g : g + 1, :]), none)
                    for m in range(2)
                ],
                axis=0,
            )
            for g in range(at, at + 8)
        ]
        sums += lax.dot_general(
            jnp.concatenate([both[g] for g in range(at, at + 8)], axis=1),
            jnp.concatenate(chosen, axis=1),
            (((1,), (1,)), ((), ())),
            preferred_element_type=jnp.float32,
        )
    sums = sums[:8] + sums[8:]
    totals[0:8, :] = sums[:, :256]
    totals[8:16, :] = sums[:, 256:]


def finish(codes, row_scale, decoded, parts, got):
    half, width = got.shape
    rows = 2 * half
    return pl.pallas_call(
        finish_kernel,
        out_shape=(jax.ShapeDtypeStruct((rows, width), jnp.float32), jax.ShapeDtypeStruct((17, 256), jnp.float32)),
        in_specs=[pl.BlockSpec(memory_space=pltpu.VMEM)] * (4 + len(parts)),
        out_specs=(pl.BlockSpec(memory_space=pltpu.VMEM),) * 2,
        compiler_params=pltpu.CompilerParams(vmem_limit_bytes=16 * 2**20),
        cost_estimate=pl.CostEstimate(flops=2**32, bytes_accessed=2**21, transcendentals=0),
        name="finish",
    )(codes, row_scale.reshape(1, rows), decoded, *parts, got)

DEPTH = 512


def tile_copies(tiles, hess, sem):
    copies = []
    for tile in tiles:
        for at in range(0, tile.shape[0], DEPTH):
            n = len(copies)
            copies.append(
                pltpu.make_async_copy(
                    tile.at[pl.ds(at, DEPTH)], hess.at[pl.ds(n * DEPTH, DEPTH)], sem.at[n]
                )
            )
    return copies


def multiply(held, hess, copies):
    total = None
    for n, copy in enumerate(copies):
        copy.wait()
        rows = slice(n * DEPTH, (n + 1) * DEPTH)
        term = jnp.dot(held[:, rows], hess[rows], preferred_element_type=jnp.float32)
        total = term if total is None else total + term
    return total.reshape(4, -1, hess.shape[1])


def first_kernel(own, far, *refs):
    blocks = refs[:-4]
    out, held, hess, sem = refs[-4:]
    width = own.shape[1]
    fetched = tile_copies((own, far), hess, sem)
    fetched[0].start()
    z_lo, y_hi, y_lo, x, z_hi, core = (lax.axis_index(a) for a in AXES)
    step = 1 - 2 * core
    copies = []
    for at, (dx, dzs) in enumerate((dx, dzs) for dzs in ((0,), (1,), (3,), (2,)) for dx in (0, 1, 3, 2)):
        for place, dz in enumerate(dzs):
            from_x = (x + 8 - step * dx) % 4
            from_z = (z_hi + 8 - step * dz) % 4
            s = (from_x + 8 - 2 * z_lo - y_hi) % 4
            tile = (from_z // 2 + y_lo) % 2
            for side in range(2):
                n = len(copies)
                part = tile * 4 + (from_z % 2) * 2 + (core + side) % 2
                rows = pl.multiple_of(s * 128, 128)
                columns = pl.multiple_of(part * width, width)
                copies.append(
                    pltpu.make_async_copy(
                        blocks[at].at[place, side],
                        held.at[pl.ds(rows, 128), pl.ds(columns, width)],
                        sem.at[len(fetched) + n],
                    )
                )
                copies[-1].start()
    for copy in fetched[1:]:
        copy.start()
    for copy in copies:
        copy.wait()
    out[...] = multiply(held, hess, fetched)


def second_kernel(kept, held, across, far_across, own, to_y, to_z, to_both, given, hess, sem):
    fetched = tile_copies((across, far_across), hess, sem)
    for copy in fetched:
        copy.start()
    given[...] = multiply(held, hess, fetched)
    width = hess.shape[1]
    z_lo, y_hi = lax.axis_index("z_lo"), lax.axis_index("y_hi")
    for out, s in (
        (own, z_lo * 2 + y_hi),
        (to_y, z_lo * 2 + 1 - y_hi),
        (to_z, (1 - z_lo) * 2 + y_hi),
        (to_both, (1 - z_lo) * 2 + 1 - y_hi),
    ):
        out[:, :width] = kept[s].astype(out.dtype)
        out[:, width:] = given[s].astype(out.dtype)


def body(codes, codebooks, row_scale, initial, hessian):
    rows, width = initial.shape
    words = codebooks.shape[1]
    codes, codebooks = jnp.swapaxes(codes, 1, 2), jnp.swapaxes(codebooks, 1, 2)
    half = rows // 2

    across = shift(hessian, "core", 1)

    decoded, mine, other = decode(codes, codebooks, row_scale, initial)
    same = send(mine, to_plane)
    cross = send(other, lambda *p: to_plane(*p)[:-1] + (1 - p[-1],))
    block = jnp.stack([same, cross])

    tile, block, across = lax.optimization_barrier((hessian, block, across))
    far = shift(tile, "y_lo", 1)

    own = block[None]
    back, on = turn(own, "z_hi", 1), turn(own, "z_hi", -1)
    last = turn(back, "z_hi", 1)
    own_back, own_on = turn(own, "x", 1), turn(own, "x", -1)
    own_two = turn(own_back, "x", 1)
    back, own_back, own_on = lax.optimization_barrier((back, own_back, own_on))
    back_back, back_on = turn(back, "x", 1), turn(back, "x", -1)
    on, own_two = lax.optimization_barrier((on, own_two))
    on_back, on_on = turn(on, "x", 1), turn(on, "x", -1)
    back_back, back_on = lax.optimization_barrier((back_back, back_on))
    back_two = turn(back_back, "x", 1)
    last_back, last_on = turn(last, "x", 1), turn(last, "x", -1)
    on_back, on_on, last_on, last_back, back_two = lax.optimization_barrier((on_back, on_on, last_on, last_back, back_two))
    on_two = turn(on_back, "x", 1)
    last_two = turn(last_back, "x", 1)
    far, *_ = lax.optimization_barrier((far, back_two, on_two, last_two))
    far_across = shift(far, "core", 1)
    wide = (
        (own, own_back, own_on, own_two),
        (back, back_back, back_on, back_two),
        (on, on_back, on_on, on_two),
        (last, last_back, last_on, last_two),
    )

    blocks = [b for group in wide for b in group]
    hbm, vmem = pl.BlockSpec(memory_space=pl.ANY), pl.BlockSpec(memory_space=pltpu.VMEM)
    settings = dict(
        compiler_params=pltpu.CompilerParams(vmem_limit_bytes=20 * 2**20),
        cost_estimate=pl.CostEstimate(
            flops=2 * 512 * 4096 * 512, bytes_accessed=8 * 2**20, transcendentals=0
        ),
    )
    kept, held = pl.pallas_call(
        first_kernel,
        out_shape=(
            jax.ShapeDtypeStruct((4, half, width), jnp.float32),
            jax.ShapeDtypeStruct((4 * half, 8 * width), jnp.bfloat16),
        ),
        in_specs=[hbm] * (2 + len(blocks)),
        out_specs=(vmem, vmem),
        scratch_shapes=[
            pltpu.VMEM((8 * width, width), jnp.bfloat16),
            pltpu.SemaphoreType.DMA((40,)),
        ],
        name="first",
        **settings,
    )(pltpu.with_memory_space_constraint(hessian, pltpu.HBM), far, *blocks)
    sent = jax.ShapeDtypeStruct((half, 2 * width), jnp.bfloat16)
    own, to_y, to_z, to_both = pl.pallas_call(
        second_kernel,
        out_shape=(jax.ShapeDtypeStruct(sent.shape, jnp.float32), sent, sent, sent),
        in_specs=[vmem, vmem, hbm, hbm],
        out_specs=(vmem,) * 4,
        scratch_shapes=[
            pltpu.VMEM((4, half, width), jnp.float32),
            pltpu.VMEM((8 * width, width), jnp.bfloat16),
            pltpu.SemaphoreType.DMA((8,)),
        ],
        name="second",
        **settings,
    )(kept, held, across, far_across)

    parts = [
        own,
        send(to_both, lambda zl, yh, yl, x, zh, c: (1 - zl, 1 - yh, yl, x, zh, c)),
        shift(to_y, "y_hi", 1),
        shift(to_z, "z_lo", 1),
    ]
    given = sum(part[:, width:].astype(jnp.float32) for part in parts)
    got = shift(given, "core", 1)
    product, total = finish(codes, row_scale, decoded, parts, got)

    total = total + shift(total, "core", 1)
    total = total + shift(total, "x", 1) + shift(total, "x", -1) + shift(total, "x", 2)
    copies = jnp.broadcast_to(total, (8, *total.shape))
    copies = lax.all_to_all(copies, ("z_hi", "z_lo"), 0, 0, tiled=True)
    scales = copies[:, 16].reshape(4, 2, rows)
    scale_total = jnp.sum(jnp.where(lax.axis_index("z_lo") == 0, scales[:, 0], scales[:, 1]), axis=0)
    books = jnp.sum(copies[:, :16], axis=0)
    beside, across_y = shift(books, "y_lo", 1), shift(books, "y_hi", 1)
    both = send(books, lambda zl, yh, yl, x, zh, c: (zl, 1 - yh, 1 - yl, x, zh, c))
    books = books + beside + across_y + both
    full_width = width * 32
    all_groups = rows * 8 * (full_width // 8)
    scale_grad = scale_total / full_width
    codebook_grad = jnp.swapaxes(books.reshape(2, 8, words), 1, 2) * (words / all_groups)
    return (product, scale_grad, codebook_grad)


def solution(mesh):
    grid = Mesh(mesh.devices.reshape(SIZES), AXES)
    in_specs = (P(None, ROW, COL), P(), P(ROW), P(ROW, COL), P(ROW, COL))
    out_specs = (P(ROW, COL), P(ROW), P())
    return jax.shard_map(body, mesh=grid, in_specs=in_specs, out_specs=out_specs, check_vma=False)
```

```python
import jax
import jax.numpy as jnp
import numpy as np
from jax import lax
from jax.experimental import pallas as pl
from jax.experimental.pallas import tpu as pltpu
from jax.sharding import Mesh
from jax.sharding import PartitionSpec as P

AXES = ("z_lo", "y_hi", "y_lo", "x", "z_hi", "core")
SIZES = (2, 2, 2, 4, 4, 2)
ROW = ("z_lo", "y_hi", "y_lo")
COL = ("x", "z_hi", "core")
PLACES = np.arange(256).reshape(SIZES)


def send(a, target):
    pairs = []
    for place in np.ndindex(*SIZES):
        to = tuple(t % n for t, n in zip(target(*place), SIZES))
        pairs.append((int(PLACES[place]), int(PLACES[to])))
    assert len({d for _, d in pairs}) == PLACES.size
    return lax.ppermute(a, AXES, pairs)


def shift(a, axis, by):
    at = AXES.index(axis)
    return send(a, lambda *p: p[:at] + (p[at] + by,) + p[at + 1 :])


def turn(a, axis, by):
    at = AXES.index(axis)
    return send(a, lambda *p: p[:at] + (p[at] + by * (1 - 2 * p[-1]),) + p[at + 1 :])


def to_plane(z_lo, y_hi, y_lo, x, z_hi, core):
    return (x // 2, x % 2, y_lo, x + 2 * z_lo + y_hi, z_hi, core)


def decode_kernel(
    codes_in, books_in, scale, initial_in, decoded, mine, other, codes, books, initial, error, sem
):
    copies = [
        pltpu.make_async_copy(a, b, sem.at[i])
        for i, (a, b) in enumerate(
            ((codes_in, codes), (books_in, books), (initial_in, initial))
        )
    ]
    for copy in copies:
        copy.start()
    copies[0].wait()
    picks = [codes[m] for m in range(2)]
    copies[1].wait()
    tables = [books[m].astype(jnp.float32) for m in range(2)]
    rows = initial.shape[0]
    for g in range(picks[0].shape[0]):
        for lane in range(0, rows, 128):
            total = None
            for m in range(2):
                word = jnp.broadcast_to(picks[m][g : g + 1, lane : lane + 128], (8, 128))
                low = word & 127
                found = [
                    jnp.take_along_axis(
                        tables[m][:, at : at + 128], low, axis=1, mode="promise_in_bounds"
                    )
                    for at in (0, 128)
                ]
                found = jnp.where(word < 128, *found)
                total = found if total is None else total + found
            decoded[8 * g : 8 * g + 8, lane : lane + 128] = total
    copies[2].wait()
    error[...] = (scale[...] * decoded[...]).T - initial[...].astype(jnp.float32)
    half = rows // 2
    core = lax.axis_index("core")
    mine[...] = error[pl.ds(pl.multiple_of(core * half, half), half)].astype(mine.dtype)
    other[...] = error[pl.ds(pl.multiple_of((1 - core) * half, half), half)].astype(mine.dtype)


def decode(codes, codebooks, row_scale, initial):
    rows, width = initial.shape
    return pl.pallas_call(
        decode_kernel,
        out_shape=(
            jax.ShapeDtypeStruct((width, rows), jnp.float32),
            jax.ShapeDtypeStruct((rows // 2, width), jnp.bfloat16),
            jax.ShapeDtypeStruct((rows // 2, width), jnp.bfloat16),
        ),
        in_specs=[
            pl.BlockSpec(memory_space=pl.ANY),
            pl.BlockSpec(memory_space=pl.ANY),
            pl.BlockSpec(memory_space=pltpu.VMEM),
            pl.BlockSpec(memory_space=pl.ANY),
        ],
        out_specs=(pl.BlockSpec(memory_space=pltpu.VMEM),) * 3,
        scratch_shapes=[
            pltpu.VMEM(codes.shape, codes.dtype),
            pltpu.VMEM(codebooks.shape, codebooks.dtype),
            pltpu.VMEM(initial.shape, initial.dtype),
            pltpu.VMEM(initial.shape, jnp.float32),
            pltpu.SemaphoreType.DMA((3,)),
        ],
        compiler_params=pltpu.CompilerParams(vmem_limit_bytes=60 * 2**20),
        cost_estimate=pl.CostEstimate(flops=2**21, bytes_accessed=2**20, transcendentals=0),
        name="decode",
    )(codes, codebooks, row_scale.reshape(1, rows), initial)


def finish_kernel(codes, scale, decoded, own, to_both, to_y, to_z, got, product, totals):
    half, width = got.shape
    kept = own[:, :width]
    for part in (to_both, to_y, to_z):
        kept = kept + part[:, :width].astype(jnp.float32)
    first = lax.axis_index("core") == 0
    product[:half] = 2.0 * jnp.where(first, kept, got[...])
    product[half:] = 2.0 * jnp.where(first, got[...], kept)
    rows, width = product.shape
    turned = product[...].T
    totals[16:17, :] = jnp.sum(turned * decoded[...], axis=0, keepdims=True)
    weighted = (turned * scale[...]).reshape(width // 8, 8, rows)
    high = weighted.astype(jnp.bfloat16).astype(jnp.float32)
    both = jnp.concatenate([high, weighted - high], axis=1).astype(jnp.bfloat16)
    picks = [codes[m].astype(jnp.bfloat16) for m in range(2)]
    words = lax.broadcasted_iota(jnp.int32, (256, rows), 0).astype(jnp.bfloat16)
    one, none = jnp.bfloat16(1), jnp.bfloat16(0)
    sums = jnp.zeros((16, 512), jnp.float32)
    for at in range(0, width // 8, 8):
        chosen = [
            jnp.concatenate(
                [
                    jnp.maximum(one - jnp.abs(words - picks[m][g : g + 1, :]), none)
                    for m in range(2)
                ],
                axis=0,
            )
            for g in range(at, at + 8)
        ]
        sums += lax.dot_general(
            jnp.concatenate([both[g] for g in range(at, at + 8)], axis=1),
            jnp.concatenate(chosen, axis=1),
            (((1,), (1,)), ((), ())),
            preferred_element_type=jnp.float32,
        )
    sums = sums[:8] + sums[8:]
    totals[0:8, :] = sums[:, :256]
    totals[8:16, :] = sums[:, 256:]


def finish(codes, row_scale, decoded, parts, got):
    half, width = got.shape
    rows = 2 * half
    return pl.pallas_call(
        finish_kernel,
        out_shape=(jax.ShapeDtypeStruct((rows, width), jnp.float32), jax.ShapeDtypeStruct((17, 256), jnp.float32)),
        in_specs=[pl.BlockSpec(memory_space=pltpu.VMEM)] * (4 + len(parts)),
        out_specs=(pl.BlockSpec(memory_space=pltpu.VMEM),) * 2,
        compiler_params=pltpu.CompilerParams(vmem_limit_bytes=16 * 2**20),
        cost_estimate=pl.CostEstimate(flops=2**32, bytes_accessed=2**21, transcendentals=0),
        name="finish",
    )(codes, row_scale.reshape(1, rows), decoded, *parts, got)

DEPTH = 512


def tile_copies(tiles, hess, sem):
    copies = []
    for tile in tiles:
        for at in range(0, tile.shape[0], DEPTH):
            n = len(copies)
            copies.append(
                pltpu.make_async_copy(
                    tile.at[pl.ds(at, DEPTH)], hess.at[pl.ds(n * DEPTH, DEPTH)], sem.at[n]
                )
            )
    return copies


def multiply(held, hess, copies):
    total = None
    for n, copy in enumerate(copies):
        copy.wait()
        rows = slice(n * DEPTH, (n + 1) * DEPTH)
        term = jnp.dot(held[:, rows], hess[rows], preferred_element_type=jnp.float32)
        total = term if total is None else total + term
    return total.reshape(4, -1, hess.shape[1])


def first_kernel(own, far, *refs):
    blocks = refs[:-4]
    out, held, hess, sem = refs[-4:]
    width = own.shape[1]
    fetched = tile_copies((own, far), hess, sem)
    fetched[0].start()
    z_lo, y_hi, y_lo, x, z_hi, core = (lax.axis_index(a) for a in AXES)
    step = 1 - 2 * core
    copies = []
    for at, (dx, dzs) in enumerate((dx, dzs) for dzs in ((0,), (1, 3), (2,)) for dx in (0, 1, 3, 2)):
        for place, dz in enumerate(dzs):
            from_x = (x + 8 - step * dx) % 4
            from_z = (z_hi + 8 - step * dz) % 4
            s = (from_x + 8 - 2 * z_lo - y_hi) % 4
            tile = (from_z // 2 + y_lo) % 2
            for side in range(2):
                n = len(copies)
                part = tile * 4 + (from_z % 2) * 2 + (core + side) % 2
                rows = pl.multiple_of(s * 128, 128)
                columns = pl.multiple_of(part * width, width)
                copies.append(
                    pltpu.make_async_copy(
                        blocks[at].at[place, side],
                        held.at[pl.ds(rows, 128), pl.ds(columns, width)],
                        sem.at[len(fetched) + n],
                    )
                )
                copies[-1].start()
    for copy in fetched[1:]:
        copy.start()
    for copy in copies:
        copy.wait()
    out[...] = multiply(held, hess, fetched)


def second_kernel(kept, held, across, far_across, own, to_y, to_z, to_both, given, hess, sem):
    fetched = tile_copies((across, far_across), hess, sem)
    for copy in fetched:
        copy.start()
    given[...] = multiply(held, hess, fetched)
    width = hess.shape[1]
    z_lo, y_hi = lax.axis_index("z_lo"), lax.axis_index("y_hi")
    for out, s in (
        (own, z_lo * 2 + y_hi),
        (to_y, z_lo * 2 + 1 - y_hi),
        (to_z, (1 - z_lo) * 2 + y_hi),
        (to_both, (1 - z_lo) * 2 + 1 - y_hi),
    ):
        out[:, :width] = kept[s].astype(out.dtype)
        out[:, width:] = given[s].astype(out.dtype)


def gather_sum(total, axes, kept):
    sizes = [lax.axis_size(a) for a in axes]
    copies = jnp.broadcast_to(total, (int(np.prod(sizes)), *total.shape))
    copies = lax.all_to_all(copies, axes, 0, 0, tiled=True)
    own = 0
    for a in kept:
        own = own * lax.axis_size(a) + lax.axis_index(a)
    behind = int(np.prod(sizes[len(kept) :]))
    source = lax.broadcasted_iota(jnp.int32, copies.shape, 0) // behind
    row = lax.broadcasted_iota(jnp.int32, copies.shape, 1)
    counts = (row < total.shape[0] - 1) | (source == own)
    return jnp.sum(jnp.where(counts, copies, 0.0), axis=0)


def body(codes, codebooks, row_scale, initial, hessian):
    rows, width = initial.shape
    words = codebooks.shape[1]
    codes, codebooks = jnp.swapaxes(codes, 1, 2), jnp.swapaxes(codebooks, 1, 2)
    half = rows // 2

    across = shift(hessian, "core", 1)

    decoded, mine, other = decode(codes, codebooks, row_scale, initial)
    same = send(mine, to_plane)
    cross = send(other, lambda *p: to_plane(*p)[:-1] + (1 - p[-1],))
    block = jnp.stack([same, cross])

    tile, block, across = lax.optimization_barrier((hessian, block, across))
    far = shift(tile, "y_lo", 1)

    own = block[None]
    z_back, z_on = turn(block, "z_hi", 1), turn(block, "z_hi", -1)
    own_back, own_on = turn(own, "x", 1), turn(own, "x", -1)
    own_two = turn(own_back, "x", 1)
    near, own_on, own_two = lax.optimization_barrier(
        (jnp.stack([z_back, z_on]), own_on, own_two)
    )
    near_back, near_on = turn(near, "x", 1), turn(near, "x", -1)
    last = turn(z_back, "z_hi", 1)[None]
    last_back, last_on = turn(last, "x", 1), turn(last, "x", -1)
    near_on, last_back, last_on, own_two = lax.optimization_barrier((near_on, last_back, last_on, own_two))
    near_two, last_two = turn(near_back, "x", 1), turn(last_back, "x", 1)
    far, near_two, last_two = lax.optimization_barrier((far, near_two, last_two))
    far_across = shift(far, "core", 1)
    wide = (
        (own, own_back, own_on, own_two),
        (near, near_back, near_on, near_two),
        (last, last_back, last_on, last_two),
    )

    blocks = [b for group in wide for b in group]
    hbm, vmem = pl.BlockSpec(memory_space=pl.ANY), pl.BlockSpec(memory_space=pltpu.VMEM)
    settings = dict(
        compiler_params=pltpu.CompilerParams(vmem_limit_bytes=20 * 2**20),
        cost_estimate=pl.CostEstimate(
            flops=2 * 512 * 4096 * 512, bytes_accessed=8 * 2**20, transcendentals=0
        ),
    )
    kept, held = pl.pallas_call(
        first_kernel,
        out_shape=(
            jax.ShapeDtypeStruct((4, half, width), jnp.float32),
            jax.ShapeDtypeStruct((4 * half, 8 * width), jnp.bfloat16),
        ),
        in_specs=[hbm] * (2 + len(blocks)),
        out_specs=(vmem, vmem),
        scratch_shapes=[
            pltpu.VMEM((8 * width, width), jnp.bfloat16),
            pltpu.SemaphoreType.DMA((40,)),
        ],
        name="first",
        **settings,
    )(pltpu.with_memory_space_constraint(hessian, pltpu.HBM), far, *blocks)
    sent = jax.ShapeDtypeStruct((half, 2 * width), jnp.bfloat16)
    own, to_y, to_z, to_both = pl.pallas_call(
        second_kernel,
        out_shape=(jax.ShapeDtypeStruct(sent.shape, jnp.float32), sent, sent, sent),
        in_specs=[vmem, vmem, hbm, hbm],
        out_specs=(vmem,) * 4,
        scratch_shapes=[
            pltpu.VMEM((4, half, width), jnp.float32),
            pltpu.VMEM((8 * width, width), jnp.bfloat16),
            pltpu.SemaphoreType.DMA((8,)),
        ],
        name="second",
        **settings,
    )(kept, held, across, far_across)

    parts = [
        own,
        send(to_both, lambda zl, yh, yl, x, zh, c: (1 - zl, 1 - yh, yl, x, zh, c)),
        shift(to_y, "y_hi", 1),
        shift(to_z, "z_lo", 1),
    ]
    given = sum(part[:, width:].astype(jnp.float32) for part in parts)
    got = shift(given, "core", 1)
    product, total = finish(codes, row_scale, decoded, parts, got)

    total = total + shift(total, "core", 1)
    total = gather_sum(total, ("y_hi", "y_lo", "x"), ("y_hi", "y_lo"))
    total = gather_sum(total, ("z_lo", "z_hi"), ("z_lo",))
    scale_total, books = total[16], total[:16]
    full_width = width * 32
    all_groups = rows * 8 * (full_width // 8)
    scale_grad = scale_total / full_width
    codebook_grad = jnp.swapaxes(books.reshape(2, 8, words), 1, 2) * (words / all_groups)
    return (product, scale_grad, codebook_grad)


def solution(mesh):
    grid = Mesh(mesh.devices.reshape(SIZES), AXES)
    in_specs = (P(None, ROW, COL), P(), P(ROW), P(ROW, COL), P(ROW, COL))
    out_specs = (P(ROW, COL), P(ROW), P())
    return jax.shard_map(body, mesh=grid, in_specs=in_specs, out_specs=out_specs, check_vma=False)
```

```python
import jax
import jax.numpy as jnp
import numpy as np
from jax import lax
from jax.experimental import pallas as pl
from jax.experimental.pallas import tpu as pltpu
from jax.sharding import Mesh
from jax.sharding import PartitionSpec as P

AXES = ("z_lo", "y_hi", "y_lo", "x", "z_hi", "core")
SIZES = (2, 2, 2, 4, 4, 2)
ROW = ("z_lo", "y_hi", "y_lo")
COL = ("x", "z_hi", "core")
PLACES = np.arange(256).reshape(SIZES)


def send(a, target):
    pairs = []
    for place in np.ndindex(*SIZES):
        to = tuple(t % n for t, n in zip(target(*place), SIZES))
        pairs.append((int(PLACES[place]), int(PLACES[to])))
    assert len({d for _, d in pairs}) == PLACES.size
    return lax.ppermute(a, AXES, pairs)


def shift(a, axis, by):
    at = AXES.index(axis)
    return send(a, lambda *p: p[:at] + (p[at] + by,) + p[at + 1 :])


def turn(a, axis, by):
    at = AXES.index(axis)
    return send(a, lambda *p: p[:at] + (p[at] + by * (1 - 2 * p[-1]),) + p[at + 1 :])


def to_plane(z_lo, y_hi, y_lo, x, z_hi, core):
    return (x // 2, x % 2, y_lo, x + 2 * z_lo + y_hi, z_hi, core)


def decode_kernel(
    codes_in, books_in, scale, initial_in, decoded, mine, other, codes, books, initial, error, sem
):
    copies = [
        pltpu.make_async_copy(a, b, sem.at[i])
        for i, (a, b) in enumerate(
            ((codes_in, codes), (books_in, books), (initial_in, initial))
        )
    ]
    for copy in copies:
        copy.start()
    copies[0].wait()
    picks = [codes[m] for m in range(2)]
    copies[1].wait()
    tables = [books[m].astype(jnp.float32) for m in range(2)]
    rows = initial.shape[0]
    for g in range(picks[0].shape[0]):
        for lane in range(0, rows, 128):
            total = None
            for m in range(2):
                word = jnp.broadcast_to(picks[m][g : g + 1, lane : lane + 128], (8, 128))
                low = word & 127
                found = [
                    jnp.take_along_axis(
                        tables[m][:, at : at + 128], low, axis=1, mode="promise_in_bounds"
                    )
                    for at in (0, 128)
                ]
                found = jnp.where(word < 128, *found)
                total = found if total is None else total + found
            decoded[8 * g : 8 * g + 8, lane : lane + 128] = total
    copies[2].wait()
    error[...] = (scale[...] * decoded[...]).T - initial[...].astype(jnp.float32)
    half = rows // 2
    core = lax.axis_index("core")
    mine[...] = error[pl.ds(pl.multiple_of(core * half, half), half)].astype(mine.dtype)
    other[...] = error[pl.ds(pl.multiple_of((1 - core) * half, half), half)].astype(mine.dtype)


def decode(codes, codebooks, row_scale, initial):
    rows, width = initial.shape
    return pl.pallas_call(
        decode_kernel,
        out_shape=(
            jax.ShapeDtypeStruct((width, rows), jnp.float32),
            jax.ShapeDtypeStruct((rows // 2, width), jnp.bfloat16),
            jax.ShapeDtypeStruct((rows // 2, width), jnp.bfloat16),
        ),
        in_specs=[
            pl.BlockSpec(memory_space=pl.ANY),
            pl.BlockSpec(memory_space=pl.ANY),
            pl.BlockSpec(memory_space=pltpu.VMEM),
            pl.BlockSpec(memory_space=pl.ANY),
        ],
        out_specs=(pl.BlockSpec(memory_space=pltpu.VMEM),) * 3,
        scratch_shapes=[
            pltpu.VMEM(codes.shape, codes.dtype),
            pltpu.VMEM(codebooks.shape, codebooks.dtype),
            pltpu.VMEM(initial.shape, initial.dtype),
            pltpu.VMEM(initial.shape, jnp.float32),
            pltpu.SemaphoreType.DMA((3,)),
        ],
        compiler_params=pltpu.CompilerParams(vmem_limit_bytes=60 * 2**20),
        cost_estimate=pl.CostEstimate(flops=2**21, bytes_accessed=2**20, transcendentals=0),
        name="decode",
    )(codes, codebooks, row_scale.reshape(1, rows), initial)


def finish_kernel(codes, scale, decoded, own, to_both, to_y, to_z, got, product, totals):
    half, width = got.shape
    kept = own[:, :width]
    for part in (to_both, to_y, to_z):
        kept = kept + part[:, :width].astype(jnp.float32)
    first = lax.axis_index("core") == 0
    product[:half] = 2.0 * jnp.where(first, kept, got[...])
    product[half:] = 2.0 * jnp.where(first, got[...], kept)
    rows, width = product.shape
    turned = product[...].T
    totals[16:17, :] = jnp.sum(turned * decoded[...], axis=0, keepdims=True)
    weighted = (turned * scale[...]).reshape(width // 8, 8, rows)
    high = weighted.astype(jnp.bfloat16).astype(jnp.float32)
    both = jnp.concatenate([high, weighted - high], axis=1).astype(jnp.bfloat16)
    picks = [codes[m].astype(jnp.bfloat16) for m in range(2)]
    words = lax.broadcasted_iota(jnp.int32, (256, rows), 0).astype(jnp.bfloat16)
    one, none = jnp.bfloat16(1), jnp.bfloat16(0)
    sums = jnp.zeros((16, 512), jnp.float32)
    for at in range(0, width // 8, 8):
        chosen = [
            jnp.concatenate(
                [
                    jnp.maximum(one - jnp.abs(words - picks[m][g : g + 1, :]), none)
                    for m in range(2)
                ],
                axis=0,
            )
            for g in range(at, at + 8)
        ]
        sums += lax.dot_general(
            jnp.concatenate([both[g] for g in range(at, at + 8)], axis=1),
            jnp.concatenate(chosen, axis=1),
            (((1,), (1,)), ((), ())),
            preferred_element_type=jnp.float32,
        )
    sums = sums[:8] + sums[8:]
    totals[0:8, :] = sums[:, :256]
    totals[8:16, :] = sums[:, 256:]


def finish(codes, row_scale, decoded, parts, got):
    half, width = got.shape
    rows = 2 * half
    return pl.pallas_call(
        finish_kernel,
        out_shape=(jax.ShapeDtypeStruct((rows, width), jnp.float32), jax.ShapeDtypeStruct((17, 256), jnp.float32)),
        in_specs=[pl.BlockSpec(memory_space=pltpu.VMEM)] * (4 + len(parts)),
        out_specs=(pl.BlockSpec(memory_space=pltpu.VMEM),) * 2,
        compiler_params=pltpu.CompilerParams(vmem_limit_bytes=16 * 2**20),
        cost_estimate=pl.CostEstimate(flops=2**32, bytes_accessed=2**21, transcendentals=0),
        name="finish",
    )(codes, row_scale.reshape(1, rows), decoded, *parts, got)

DEPTH = 512


def tile_copies(tiles, hess, sem):
    copies = []
    for tile in tiles:
        for at in range(0, tile.shape[0], DEPTH):
            n = len(copies)
            copies.append(
                pltpu.make_async_copy(
                    tile.at[pl.ds(at, DEPTH)], hess.at[pl.ds(n * DEPTH, DEPTH)], sem.at[n]
                )
            )
    return copies


def multiply(held, hess, copies):
    total = None
    for n, copy in enumerate(copies):
        copy.wait()
        rows = slice(n * DEPTH, (n + 1) * DEPTH)
        term = jnp.dot(held[:, rows], hess[rows], preferred_element_type=jnp.float32)
        total = term if total is None else total + term
    return total.reshape(4, -1, hess.shape[1])


def first_kernel(own, far, *refs):
    blocks = refs[:-4]
    out, held, hess, sem = refs[-4:]
    width = own.shape[1]
    fetched = tile_copies((own, far), hess, sem)
    fetched[0].start()
    z_lo, y_hi, y_lo, x, z_hi, core = (lax.axis_index(a) for a in AXES)
    step = 1 - 2 * core
    copies = []
    for at, (dx, dzs) in enumerate((dx, dzs) for dzs in ((0,), (1, 3), (2,)) for dx in (0, 1, 3, 2)):
        for place, dz in enumerate(dzs):
            from_x = (x + 8 - step * dx) % 4
            from_z = (z_hi + 8 - step * dz) % 4
            s = (from_x + 8 - 2 * z_lo - y_hi) % 4
            tile = (from_z // 2 + y_lo) % 2
            for side in range(2):
                n = len(copies)
                part = tile * 4 + (from_z % 2) * 2 + (core + side) % 2
                rows = pl.multiple_of(s * 128, 128)
                columns = pl.multiple_of(part * width, width)
                copies.append(
                    pltpu.make_async_copy(
                        blocks[at].at[place, side],
                        held.at[pl.ds(rows, 128), pl.ds(columns, width)],
                        sem.at[len(fetched) + n],
                    )
                )
                copies[-1].start()
    for copy in fetched[1:]:
        copy.start()
    for copy in copies:
        copy.wait()
    out[...] = multiply(held, hess, fetched)


def second_kernel(kept, held, across, far_across, own, to_y, to_z, to_both, given, hess, sem):
    fetched = tile_copies((across, far_across), hess, sem)
    for copy in fetched:
        copy.start()
    given[...] = multiply(held, hess, fetched)
    width = hess.shape[1]
    z_lo, y_hi = lax.axis_index("z_lo"), lax.axis_index("y_hi")
    for out, s in (
        (own, z_lo * 2 + y_hi),
        (to_y, z_lo * 2 + 1 - y_hi),
        (to_z, (1 - z_lo) * 2 + y_hi),
        (to_both, (1 - z_lo) * 2 + 1 - y_hi),
    ):
        out[:, :width] = kept[s].astype(out.dtype)
        out[:, width:] = given[s].astype(out.dtype)


def gather_sum(total, axes, kept):
    sizes = [lax.axis_size(a) for a in axes]
    copies = jnp.broadcast_to(total, (int(np.prod(sizes)), *total.shape))
    copies = lax.all_to_all(copies, axes, 0, 0, tiled=True)
    own = 0
    for a in kept:
        own = own * lax.axis_size(a) + lax.axis_index(a)
    behind = int(np.prod(sizes[len(kept) :]))
    source = lax.broadcasted_iota(jnp.int32, copies.shape, 0) // behind
    row = lax.broadcasted_iota(jnp.int32, copies.shape, 1)
    counts = (row < total.shape[0] - 1) | (source == own)
    return jnp.sum(jnp.where(counts, copies, 0.0), axis=0)


def body(codes, codebooks, row_scale, initial, hessian):
    rows, width = initial.shape
    words = codebooks.shape[1]
    codes, codebooks = jnp.swapaxes(codes, 1, 2), jnp.swapaxes(codebooks, 1, 2)
    half = rows // 2

    across = shift(hessian, "core", 1)

    decoded, mine, other = decode(codes, codebooks, row_scale, initial)
    same = send(mine, to_plane)
    cross = send(other, lambda *p: to_plane(*p)[:-1] + (1 - p[-1],))
    block = jnp.stack([same, cross])

    tile, block, across = lax.optimization_barrier((hessian, block, across))
    far = shift(tile, "y_lo", 1)

    own = block[None]
    z_back, z_on = turn(block, "z_hi", 1), turn(block, "z_hi", -1)
    own_back, own_on = turn(own, "x", 1), turn(own, "x", -1)
    own_two = turn(own_back, "x", 1)
    near, own_on, own_two = lax.optimization_barrier(
        (jnp.stack([z_back, z_on]), own_on, own_two)
    )
    near_back, near_on = turn(near, "x", 1), turn(near, "x", -1)
    last = turn(z_back, "z_hi", 1)[None]
    last_back, last_on = turn(last, "x", 1), turn(last, "x", -1)
    near_on, last_back, last_on, own_two = lax.optimization_barrier((near_on, last_back, last_on, own_two))
    near_two, last_two = turn(near_back, "x", 1), turn(last_back, "x", 1)
    far, near_two, last_two = lax.optimization_barrier((far, near_two, last_two))
    far_across = shift(far, "core", 1)
    wide = (
        (own, own_back, own_on, own_two),
        (near, near_back, near_on, near_two),
        (last, last_back, last_on, last_two),
    )

    blocks = [b for group in wide for b in group]
    hbm, vmem = pl.BlockSpec(memory_space=pl.ANY), pl.BlockSpec(memory_space=pltpu.VMEM)
    settings = dict(
        compiler_params=pltpu.CompilerParams(vmem_limit_bytes=20 * 2**20),
        cost_estimate=pl.CostEstimate(
            flops=2 * 512 * 4096 * 512, bytes_accessed=8 * 2**20, transcendentals=0
        ),
    )
    kept, held = pl.pallas_call(
        first_kernel,
        out_shape=(
            jax.ShapeDtypeStruct((4, half, width), jnp.float32),
            jax.ShapeDtypeStruct((4 * half, 8 * width), jnp.bfloat16),
        ),
        in_specs=[hbm] * (2 + len(blocks)),
        out_specs=(vmem, vmem),
        scratch_shapes=[
            pltpu.VMEM((8 * width, width), jnp.bfloat16),
            pltpu.SemaphoreType.DMA((40,)),
        ],
        name="first",
        **settings,
    )(pltpu.with_memory_space_constraint(hessian, pltpu.HBM), far, *blocks)
    sent = jax.ShapeDtypeStruct((half, 2 * width), jnp.bfloat16)
    own, to_y, to_z, to_both = pl.pallas_call(
        second_kernel,
        out_shape=(jax.ShapeDtypeStruct(sent.shape, jnp.float32), sent, sent, sent),
        in_specs=[vmem, vmem, hbm, hbm],
        out_specs=(vmem,) * 4,
        scratch_shapes=[
            pltpu.VMEM((4, half, width), jnp.float32),
            pltpu.VMEM((8 * width, width), jnp.bfloat16),
            pltpu.SemaphoreType.DMA((8,)),
        ],
        name="second",
        **settings,
    )(kept, held, across, far_across)

    parts = [
        own,
        send(to_both, lambda zl, yh, yl, x, zh, c: (1 - zl, 1 - yh, yl, x, zh, c)),
        shift(to_y, "y_hi", 1),
        shift(to_z, "z_lo", 1),
    ]
    given = sum(part[:, width:].astype(jnp.float32) for part in parts)
    got = shift(given, "core", 1)
    product, total = finish(codes, row_scale, decoded, parts, got)

    total = total + shift(total, "core", 1)
    total = total + shift(total, "x", 1) + shift(total, "x", -1) + shift(total, "x", 2)
    total = gather_sum(total, ("z_lo", "z_hi"), ("z_lo",))
    scale_total, books = total[16], total[:16]
    beside, across_y = shift(books, "y_lo", 1), shift(books, "y_hi", 1)
    both = send(books, lambda zl, yh, yl, x, zh, c: (zl, 1 - yh, 1 - yl, x, zh, c))
    books = books + beside + across_y + both
    full_width = width * 32
    all_groups = rows * 8 * (full_width // 8)
    scale_grad = scale_total / full_width
    codebook_grad = jnp.swapaxes(books.reshape(2, 8, words), 1, 2) * (words / all_groups)
    return (product, scale_grad, codebook_grad)


def solution(mesh):
    grid = Mesh(mesh.devices.reshape(SIZES), AXES)
    in_specs = (P(None, ROW, COL), P(), P(ROW), P(ROW, COL), P(ROW, COL))
    out_specs = (P(ROW, COL), P(ROW), P())
    return jax.shard_map(body, mesh=grid, in_specs=in_specs, out_specs=out_specs, check_vma=False)
```
